128 devices in a mesh: hid: 8 (over x, core), ep: 16 (over z, y).
Axes of the slice: x: 4, y: 4, z: 4, core: 2. Of those that a mesh axis runs over, the one named last changes fastest.
Arguments:
- gate_proj: bfloat16 [2, 7168, 2048], P(None, 'hid', 'ep'), may hold values from -6 to 6
- up_proj: bfloat16 [2, 7168, 2048], P(None, 'hid', 'ep'), may hold values from -6 to 6
- down_proj: bfloat16 [2, 2048, 7168], P(None, 'ep', 'hid'), may hold values from -6 to 6
- rotation: bfloat16 [7168, 7168], P('hid'), may hold values from -0.0625 to 0.0625
- placement: int32 [2, 16], replicated, may hold values from 0 to 15, each once within a row
- row_count: int32 [2, 16], replicated, may hold values from 16 to 256, as said below
Outputs:
- served: bfloat16 [16, 512, 3, 7168], P('ep', 'hid')
The draws below stay inside these ranges and needn't reach their ends.
Inputs may be any that keep to these rules, and one draw needn't show every extreme that they name: `row_count`: every count is a multiple of 16, each expert's counts sum to 2048, and one owner holds 256 rows of every expert.
All inputs are finite; a program needn't handle non-finite values.
Results may differ from the reference program's by a relative error of at most 0.017.
Values may be sent and summed in bfloat16 or wider, within the bound.
A program may use at most 128 MiB of HBM per device.

```python
import jax
import jax.numpy as jnp

H = 7168
F = 2048
EXP = 2
OWNERS = 16
HID_SHARDS = 8
BLOCKS = 128
SUB = 16
SLOTS_DEV = 64
SLOTS = 512
N_HID = 8


def draw_row_count(key, part):
    key = jax.random.fold_in(key, 7)
    key_busiest, key_spread = jax.random.split(key)
    busiest = jax.random.randint(key_busiest, (), 0, OWNERS)
    spare_room = 2 * HID_SHARDS - 1
    extra_total = BLOCKS - 2 * HID_SHARDS - (OWNERS - 1)
    tokens = jnp.repeat(jnp.arange(OWNERS - 1, dtype=jnp.int32), spare_room)

    def one_expert(sub_key):
        shuffled = jax.random.permutation(sub_key, tokens)
        taken_ids = shuffled[:extra_total]
        extra_blocks = jnp.sum((taken_ids[:, None] == jnp.arange(OWNERS - 1, dtype=jnp.int32)[None, :]).astype(jnp.int32), axis=0)
        others = 1 + extra_blocks
        owner_ids = jnp.arange(OWNERS, dtype=jnp.int32)
        other_index = jnp.clip(owner_ids - (owner_ids > busiest).astype(jnp.int32), 0, OWNERS - 2)
        return jnp.where(owner_ids == busiest, 2 * HID_SHARDS, others[other_index]) * SUB
    return jax.vmap(one_expert)(jax.random.split(key_spread, EXP)).astype(jnp.int32)


def level_of(key, extent, cuts, low, largest):
    factor_of, own = 1.0, jax.random.fold_in(key, 6)
    for dim, parts in cuts:
        draws = jnp.exp(jax.random.uniform(jax.random.fold_in(own, dim), (parts,), jnp.float32, low / len(cuts), largest / len(cuts)))
        factor_of = factor_of * jnp.repeat(draws, extent[dim] // parts).reshape([-1 if axis == dim else 1 for axis in range(len(extent))])
    return factor_of


def scatter_about(own_key, dims, deviation, most, cuts=(), held_as=jnp.bfloat16):
    values = jax.random.normal(own_key, dims, jnp.float32) * deviation
    if len(cuts) > 0:
        values = level_of(own_key, dims, cuts, -0.22, 0.18) * values
    return jnp.clip(values, min=-most, max=most).astype(held_as)


def setup_inputs(seed: int = 0) -> dict:
    seeds = jax.random.split(jax.random.key(seed), 7)
    return {
        "gate_proj": scatter_about(seeds[0], (EXP, H, F), 1.0, 6.0, ((1, 8), (2, 16))),
        "up_proj": scatter_about(seeds[1], (EXP, H, F), 1.0, 6.0, ((1, 8), (2, 16))),
        "down_proj": scatter_about(seeds[2], (EXP, F, H), 1.0, 6.0, ((1, 16), (2, 8))),
        "rotation": scatter_about(seeds[3], (H, H), H ** -0.5, 0.0625, ((0, 8),)),
        "placement": jax.vmap(lambda own: jax.random.permutation(own, OWNERS))(jax.random.split(seeds[4], EXP)).reshape((EXP, OWNERS)).astype(jnp.int32),
        "row_count": draw_row_count(jax.random.fold_in(seeds[6], 71), 0),
    }


def count_below(bound, residue, shard_total):
    return ((bound + shard_total - 1 - residue) // shard_total).astype(jnp.int32)


def routing(placement, row_count, block_rows):
    owner_total = placement.shape[1]
    blocks = (row_count // block_rows).astype(jnp.int32)
    onehot = (placement[:, :, None] == jnp.arange(owner_total, dtype=jnp.int32)[None, None, :]).astype(jnp.int32)
    ordered = jnp.sum(onehot * blocks[:, None, :], axis=2).astype(jnp.int32)
    ordered_start = (jnp.cumsum(ordered, axis=1) - ordered).astype(jnp.int32)
    first_block = jnp.sum(onehot * ordered_start[:, :, None], axis=1).astype(jnp.int32)
    return blocks, first_block


def reference(gate_proj, up_proj, down_proj, rotation, placement, row_count):
    sources = [jnp.transpose(gate_proj, (0, 2, 1)), jnp.transpose(up_proj, (0, 2, 1)), down_proj]
    piece_width = H // N_HID
    results = []
    for expert in range(EXP):
        per_kind = []
        for source in sources:
            accumulated = jnp.zeros((F, H), jnp.float32)
            for hid_block in range(N_HID):
                columns = source[expert][:, hid_block * piece_width:(hid_block + 1) * piece_width]
                term = jnp.dot(columns, rotation[hid_block * piece_width:(hid_block + 1) * piece_width], preferred_element_type=jnp.float32)
                accumulated = accumulated + term.astype(jnp.bfloat16).astype(jnp.float32)
            per_kind.append(accumulated.astype(jnp.bfloat16))
        results.append(jnp.stack(per_kind, axis=1))
    rotated = jnp.stack(results)
    blocks, first_block = routing(placement, row_count, SUB)
    block_ids = jnp.arange(BLOCKS, dtype=jnp.int32)
    residue = (block_ids % N_HID).astype(jnp.int32)
    inside = ((first_block[:, None, :] <= block_ids[None, :, None]) & (block_ids[None, :, None] < (first_block + blocks)[:, None, :])).astype(jnp.int32)
    owner_ids = jnp.arange(OWNERS, dtype=jnp.int32)
    target_owner = jnp.sum(inside * owner_ids[None, None, :], axis=2).astype(jnp.int32)
    shard_ids = jnp.arange(N_HID, dtype=jnp.int32)
    at_shard = count_below((first_block + blocks)[:, :, None], shard_ids[None, None, :], N_HID) - count_below(first_block[:, :, None], shard_ids[None, None, :], N_HID)
    offset = (jnp.cumsum(at_shard, axis=0) - at_shard).astype(jnp.int32)
    offset_here = jnp.transpose(jnp.take(offset, residue, axis=2), (0, 2, 1))
    base_here = count_below(first_block[:, None, :], residue[None, :, None], N_HID)
    slot_index = jnp.sum(inside * (offset_here - base_here), axis=2).astype(jnp.int32) + count_below(block_ids, residue, N_HID)[None, :]
    position = residue[None, :] * SLOTS_DEV + slot_index * SUB
    row_ids = position[:, :, None] + jnp.arange(SUB, dtype=jnp.int32)[None, None, :]
    owner_rows = jnp.broadcast_to(target_owner[:, :, None], row_ids.shape)
    values = rotated.reshape(EXP * F, 3, H)
    served = jnp.zeros((OWNERS, SLOTS, 3, H), jnp.bfloat16)
    served = served.at[owner_rows.reshape(-1), row_ids.reshape(-1)].set(values)
    return served
```

```python
import functools

import jax
import jax.numpy as jnp
from jax import lax
from jax.experimental import pallas as pl
from jax.experimental.pallas import tpu as pltpu
from jax.sharding import PartitionSpec as P

MESH = pl.DeviceIdType.MESH
BF = jnp.bfloat16
F32 = jnp.float32
PEERS = (
    (0, 1), (0, 3), (1, 0), (3, 0), (1, 1), (3, 3), (1, 3), (3, 1),
    (0, 2), (2, 0), (1, 2), (2, 1), (3, 2), (2, 3), (2, 2),
)
KINDS = 3
SPLIT = 2
CHUNKS = KINDS * SPLIT
WIDTH = 7168 // SPLIT
QUARTER = WIDTH // 4
TILE = 512


def onehot(rows, cols, condition):
    r = lax.broadcasted_iota(jnp.int32, (rows, cols), 0)
    s = lax.broadcasted_iota(jnp.int32, (rows, cols), 1)
    return jnp.where(condition(r, s), 1.0, 0.0).astype(BF)


def dot(a, b):
    return jnp.dot(a, b, preferred_element_type=F32)


def dot_t(a, b):
    return lax.dot_general(a, b, (((1,), (1,)), ((), ())), preferred_element_type=F32)


def owner_select(h, placement_ref, count_ref):
    owners = lax.broadcasted_iota(jnp.int32, (16, 128), 0)
    low, high = [], []
    for m in range(2):
        start = jnp.int32(0)
        lo = jnp.zeros((16, 128), jnp.int32)
        hi = jnp.zeros((16, 128), jnp.int32)
        for t in range(16):
            o = placement_ref[m, t]
            end = start + lax.shift_right_logical(count_ref[m, o], 4)
            lo = jnp.where(owners == o, lax.shift_right_logical(start + 7 - h, 3), lo)
            hi = jnp.where(owners == o, lax.shift_right_logical(end + 7 - h, 3), hi)
            start = end
        low.append(lo)
        high.append(hi)
    col = lax.broadcasted_iota(jnp.int32, (16, 128), 1)
    m = (col // 16) % 2
    e = col % 16
    lo = jnp.where(m == 0, low[0], low[1])
    hi = jnp.where(m == 0, high[0], high[1])
    slot = e - lo + jnp.where(m == 0, 0, high[0] - low[0])
    slot = jnp.where((lo <= e) & (e < hi), slot, -1)
    slot = jnp.broadcast_to(slot[:, None, :], (16, 16, 128)).reshape(256, 128)
    r = lax.broadcasted_iota(jnp.int32, (256, 128), 0)
    s = lax.broadcasted_iota(jnp.int32, (256, 128), 1)
    keep = (slot == (r // 4) % 4) & (r % 4 == s // 32)
    return jnp.where(keep, 1.0, 0.0).astype(BF)


def kernel(
    placement_ref, count_ref, gate_ref, up_ref, down_ref, rot_hbm, out_hbm,
    rot, src, rcv, lhs, core_out, core_in, own, far_left, far_right, from_left, from_right,
    sel, perm, own_out, own_in, outv,
    rot_sem, src_send, src_recv, core_send, core_recv, x_send, x_recv, own_send, own_recv, out_sem,
):
    hid = lax.axis_index("hid")
    ep = lax.axis_index("ep")
    x, core = hid // 2, hid % 2
    z, y = ep // 4, ep % 4
    right = lax.rem(x + 1, 4) * 2 + core
    left = lax.rem(x + 3, 4) * 2 + core
    other = x * 2 + 1 - core
    peers = [lax.rem(z + dz, 4) * 4 + lax.rem(y + dy, 4) for dz, dy in PEERS]

    barrier = pltpu.get_barrier_semaphore()
    for h in (right, left, other):
        pl.semaphore_signal(barrier, 1, device_id=(h, ep), device_id_type=MESH)
    for p in peers:
        pl.semaphore_signal(barrier, 1, device_id=(hid, p), device_id_type=MESH)

    rot_copy = pltpu.make_async_copy(rot_hbm, rot, rot_sem)
    rot_copy.start()

    spread = [
        onehot(256, 128, lambda r, s: ((r // 8) % 2 == m) & (s == (r % 8) * 16 + r // 16))
        for m in range(2)
    ]
    for k, ref in enumerate((gate_ref, up_ref)):
        rows = dot_t(spread[0], ref[0]) + dot_t(spread[1], ref[1])
        src[k] = rows.astype(BF).reshape(16, 16, 896)
    rows = dot(spread[0], down_ref[0]) + dot(spread[1], down_ref[1])
    src[2] = rows.astype(BF).reshape(16, 16, 896)

    pl.semaphore_wait(barrier, 3 + len(PEERS))

    def src_copy(k, i):
        return pltpu.make_async_remote_copy(
            src.at[k, peers[i]], rcv.at[k, ep], src_send.at[k, i], src_recv.at[k, i],
            device_id=(hid, peers[i]), device_id_type=MESH,
        )

    for k in range(KINDS):
        for i in range(len(PEERS)):
            src_copy(k, i).start()
    for k in range(KINDS):
        rcv[k, ep] = src[k, ep]

    sel[...] = owner_select(hid, placement_ref, count_ref)

    def arrange(r, s):
        d = (r // 32) % 4
        d = jnp.where(d == 0, 2, jnp.where(d == 1, 1, jnp.where(d == 2, 3, 0)))
        b = ((x + d) % 4) * 2 + jnp.where(r < 128, 1 - core, core)
        return s == (r % 16) * 16 + ((r // 16) % 2) * 8 + b

    perm[0] = onehot(256, 256, arrange)
    perm[1] = onehot(
        256, 256, lambda r, s: s == (r % 16) * 16 + ((r // 16) % 4) * 4 + r // 64
    )

    def core_copy(n):
        return pltpu.make_async_remote_copy(
            core_out.at[n], core_in.at[n], core_send.at[n], core_recv.at[n],
            device_id=(other, ep), device_id_type=MESH,
        )

    def x_copy(n, i):
        first, to, dst = (
            (0, right, far_left.at[n]),
            (16, left, far_right.at[n]),
            (48, right, from_left.at[n, pl.ds(16, 16)]),
            (64, left, from_right.at[n, pl.ds(0, 16)]),
            (32, right, from_left.at[n, pl.ds(0, 16)]),
            (80, left, from_right.at[n, pl.ds(16, 16)]),
        )[i]
        return pltpu.make_async_remote_copy(
            own.at[n, pl.ds(first, 16)], dst, x_send.at[n, i], x_recv.at[n, i],
            device_id=(to, ep), device_id_type=MESH,
        )

    def own_copy(n, i):
        return pltpu.make_async_remote_copy(
            own_out.at[n, peers[i]], own_in.at[n, ep], own_send.at[n, i], own_recv.at[n, i],
            device_id=(hid, peers[i]), device_id_type=MESH,
        )

    def out_copy(n):
        columns = pl.ds(pl.multiple_of((n % SPLIT) * WIDTH, 128), WIDTH)
        return pltpu.make_async_copy(outv.at[n], out_hbm.at[n // SPLIT, :, columns], out_sem.at[n])

    def add(n, first, rows, ref):
        own[n, first:first + rows] = (
            own[n, first:first + rows].astype(F32) + ref.astype(F32)
        ).astype(BF)

    def multiply(n):
        k = n // SPLIT

        @pl.when(n % SPLIT == 0)
        def _():
            for i in range(len(PEERS)):
                src_copy(k, i).wait_recv()
            lhs[k] = dot(perm[0], rcv[k].reshape(256, 896)).astype(BF)

        @pl.loop(0, WIDTH // TILE)
        def _(t):
            here = pl.ds(pl.multiple_of(t * TILE, TILE), TILE)
            there = pl.ds(pl.multiple_of((n % SPLIT) * WIDTH + t * TILE, TILE), TILE)
            total = dot(lhs[k], rot[:, there])
            core_out[n, :, here] = total[:128].astype(BF)
            own[n, :, here] = total[128:].astype(BF)

        core_copy(n).start()

    def sum_cores(n):
        core_copy(n).wait_recv()
        add(n, 0, 32, core_in[n, 0:32])
        x_copy(n, 0).start()
        x_copy(n, 1).start()
        add(n, 32, 64, core_in[n, 32:96])
        x_copy(n, 2).start()
        x_copy(n, 3).start()
        add(n, 96, 32, core_in[n, 96:128])

    def pass_on(n):
        x_copy(n, 0).wait_recv()
        add(n, 32, 16, far_left[n])
        x_copy(n, 4).start()
        x_copy(n, 1).wait_recv()
        add(n, 80, 16, far_right[n])
        x_copy(n, 5).start()

    def to_owners(n):
        for i in range(2, 6):
            x_copy(n, i).wait_recv()
        parts = []
        for g in range(4):
            at = slice(g * QUARTER, (g + 1) * QUARTER)
            parts.append((
                own[n, 96:128, at].astype(F32)
                + from_left[n, :, at].astype(F32)
                + from_right[n, :, at].astype(F32)
            ).astype(BF))
        rows = dot(sel[...], jnp.concatenate(parts, axis=0))
        own_out[n] = rows.astype(BF).reshape(16, 16, QUARTER)
        for i in range(len(PEERS)):
            own_copy(n, i).start()
        own_in[n, ep] = own_out[n, ep]

    def place(n):
        for i in range(len(PEERS)):
            own_copy(n, i).wait_recv()
        rows = dot(perm[1], own_in[n].reshape(256, QUARTER)).astype(BF)
        for g in range(4):
            outv[n, :, g * QUARTER:(g + 1) * QUARTER] = rows[g * 64:(g + 1) * 64]
        out_copy(n).start()

    rot_copy.wait()

    stages = (multiply, sum_cores, pass_on, to_owners, place)
    lags = (0, 1, 2, 3, 4)

    @pl.loop(0, CHUNKS + lags[-1])
    def _(t):
        for stage, lag in zip(stages, lags):
            @pl.when((t >= lag) & (t < CHUNKS + lag))
            def _():
                stage(t - lag)

    for k in range(KINDS):
        for i in range(len(PEERS)):
            src_copy(k, i).wait_send()

    @pl.loop(0, CHUNKS)
    def _(n):
        core_copy(n).wait_send()
        for i in range(6):
            x_copy(n, i).wait_send()
        for i in range(len(PEERS)):
            own_copy(n, i).wait_send()
        out_copy(n).wait()


def on_device(gate_proj, up_proj, down_proj, rotation, placement, row_count):
    dma = pltpu.SemaphoreType.DMA
    peers = len(PEERS)
    vmem = pl.BlockSpec(memory_space=pltpu.VMEM)
    smem = pl.BlockSpec(memory_space=pltpu.SMEM)
    hbm = pl.BlockSpec(memory_space=pl.ANY)
    out = pl.pallas_call(
        kernel,
        out_shape=jax.ShapeDtypeStruct((3, 64, 7168), BF),
        in_specs=[smem, smem, vmem, vmem, vmem, hbm],
        out_specs=hbm,
        scratch_shapes=[
            pltpu.VMEM((896, 7168), BF),
            pltpu.VMEM((KINDS, 16, 16, 896), BF),
            pltpu.VMEM((KINDS, 16, 16, 896), BF),
            pltpu.VMEM((KINDS, 256, 896), BF),
            pltpu.VMEM((CHUNKS, 128, WIDTH), BF),
            pltpu.VMEM((CHUNKS, 128, WIDTH), BF),
            pltpu.VMEM((CHUNKS, 128, WIDTH), BF),
            pltpu.VMEM((CHUNKS, 16, WIDTH), BF),
            pltpu.VMEM((CHUNKS, 16, WIDTH), BF),
            pltpu.VMEM((CHUNKS, 32, WIDTH), BF),
            pltpu.VMEM((CHUNKS, 32, WIDTH), BF),
            pltpu.VMEM((256, 128), BF),
            pltpu.VMEM((2, 256, 256), BF),
            pltpu.VMEM((CHUNKS, 16, 16, QUARTER), BF),
            pltpu.VMEM((CHUNKS, 16, 16, QUARTER), BF),
            pltpu.VMEM((CHUNKS, 64, WIDTH), BF),
            dma,
            dma((KINDS, peers)),
            dma((KINDS, peers)),
            dma((CHUNKS,)),
            dma((CHUNKS,)),
            dma((CHUNKS, 6)),
            dma((CHUNKS, 6)),
            dma((CHUNKS, peers)),
            dma((CHUNKS, peers)),
            dma((CHUNKS,)),
        ],
        compiler_params=pltpu.CompilerParams(
            collective_id=0, has_side_effects=True, vmem_limit_bytes=60 * 1024 * 1024
        ),
        name="rotate_and_place",
    )(placement, row_count, gate_proj, up_proj, down_proj, rotation)
    return jnp.transpose(out, (1, 0, 2))[None]


def solution(mesh):
    in_specs = (
        P(None, "hid", "ep"),
        P(None, "hid", "ep"),
        P(None, "ep", "hid"),
        P("hid", None),
        P(),
        P(),
    )
    out_specs = P("ep", "hid", None, None)
    return jax.shard_map(
        on_device, mesh=mesh, in_specs=in_specs, out_specs=out_specs, check_vma=False
    )
```

```python
import jax
import jax.numpy as jnp
from jax import lax
from jax.experimental import pallas as pl
from jax.experimental.pallas import tpu as pltpu
from jax.sharding import PartitionSpec as P

MESH = pl.DeviceIdType.MESH
BF = jnp.bfloat16
F32 = jnp.float32
PEERS = (
    (0, 1), (0, 3), (1, 0), (3, 0), (1, 1), (3, 3), (1, 3), (3, 1),
    (0, 2), (2, 0), (1, 2), (2, 1), (3, 2), (2, 3), (2, 2),
)
OTHERS = len(PEERS)
HIDDEN = 7168
PIECE = 896
A_WIDTHS = (1024, 2048, 4096)
A_STARTS = (0, 1024, 3072)
A_CHUNKS = len(A_WIDTHS)
B_WIDTH = 1024
B_CHUNKS = HIDDEN // B_WIDTH
B_QUARTER = B_WIDTH // 4
TILE = 1024


def iotas(rows, cols):
    return (
        lax.broadcasted_iota(jnp.int32, (rows, cols), 0),
        lax.broadcasted_iota(jnp.int32, (rows, cols), 1),
    )


def onehot(condition):
    return jnp.where(condition, 1.0, 0.0).astype(BF)


def dot(a, b):
    return jnp.dot(a, b, preferred_element_type=F32)


def dot_t(a, b):
    return lax.dot_general(a, b, (((1,), (1,)), ((), ())), preferred_element_type=F32)


def ring_offset(index):
    return jnp.where(index == 0, 2, jnp.where(index == 1, 1, jnp.where(index == 2, 3, 0)))


def ranges(h, ep, placement_ref, count_ref):
    owners, _ = iotas(16, 256)
    low, high, mine = [], [], []
    for m in range(2):
        start = jnp.int32(0)
        count = jnp.int32(0)
        lo = jnp.zeros((16, 256), jnp.int32)
        hi = jnp.zeros((16, 256), jnp.int32)
        for t in range(16):
            o = placement_ref[m, t]
            end = start + lax.shift_right_logical(count_ref[m, o], 4)
            first = lax.shift_right_logical(start + 7 - h, 3)
            last = lax.shift_right_logical(end + 7 - h, 3)
            lo = jnp.where(owners == o, first, lo)
            hi = jnp.where(owners == o, last, hi)
            count = jnp.where(o == ep, last - first, count)
            start = end
        low.append(lo)
        high.append(hi)
        mine.append(count)
    return low, high, mine


def select_a(ep, low, high):
    first = ep < 8
    lo = jnp.where(first, low[0], low[1])
    hi = jnp.where(first, high[0], high[1])
    _, col = iotas(16, 256)
    e = col // 16
    place = jnp.where((lo <= e) & (e < hi), e - lo, -1)
    place = jnp.broadcast_to(place[:, None, :], (16, 32, 256)).reshape(512, 256)
    r, s = iotas(512, 256)
    return onehot((place == (r // 16) % 2) & (r % 16 == s % 16))


def place_a(mine):
    r, s = iotas(64, 64)
    slot = (s // 16) % 2 + jnp.where(s < 32, 0, mine[0])
    return onehot((slot == r // 16) & (r % 16 == s % 16))


def select_b(low, high):
    _, col = iotas(16, 128)
    m = (col // 16) % 2
    e = col % 16
    low = [v[:, :128] for v in low]
    high = [v[:, :128] for v in high]
    lo = jnp.where(m == 0, low[0], low[1])
    hi = jnp.where(m == 0, high[0], high[1])
    slot = e - lo + jnp.where(m == 0, 0, high[0] - low[0])
    slot = jnp.where((lo <= e) & (e < hi), slot, -1)
    slot = jnp.broadcast_to(slot[:, None, :], (16, 16, 128)).reshape(256, 128)
    r, s = iotas(256, 128)
    return onehot((slot == (r // 4) % 4) & (r % 4 == s // 32))


def kernel(
    placement_ref, count_ref, gate_ref, up_ref, down_ref, rot_hbm, out_hbm, *scratch
):
    scratch = list(scratch)

    def take(count):
        taken = scratch[:count]
        del scratch[:count]
        return taken

    rot, lhs_a, lhs_b, src, rcv, sel_a, put_a, sel_b, put_b, arrange = take(10)
    a_core_out, a_core_in, a_own, a_far, a_from, a_sum, a_in, a_pick, a_got, a_out = (
        take(A_CHUNKS) for _ in range(10)
    )
    b_core_out, b_core_in, b_own, b_far, b_from, b_pick, b_got, b_out = take(8)
    rot_sem, src_send, src_recv = take(3)
    a_core_send, a_core_recv, a_x_send, a_x_recv, a_in_send, a_in_recv = take(6)
    a_own_send, a_own_recv, a_out_sem = take(3)
    b_core_send, b_core_recv, b_x_send, b_x_recv, b_own_send, b_own_recv, b_out_sem = take(7)

    hid = lax.axis_index("hid")
    ep = lax.axis_index("ep")
    x, core = hid // 2, hid % 2
    z, y = ep // 4, ep % 4
    right = lax.rem(x + 1, 4) * 2 + core
    left = lax.rem(x + 3, 4) * 2 + core
    other = x * 2 + 1 - core
    peers = [lax.rem(z + dz, 4) * 4 + lax.rem(y + dy, 4) for dz, dy in PEERS]

    def remote(source, target, send, recv, h, e):
        return pltpu.make_async_remote_copy(
            source, target, send, recv, device_id=(h, e), device_id_type=MESH
        )

    barrier = pltpu.get_barrier_semaphore()
    for h in (right, left, other):
        pl.semaphore_signal(barrier, 1, device_id=(h, ep), device_id_type=MESH)
    for p in peers:
        pl.semaphore_signal(barrier, 1, device_id=(hid, p), device_id_type=MESH)

    def rot_copy(c):
        columns = pl.ds(A_STARTS[c], A_WIDTHS[c])
        return pltpu.make_async_copy(rot_hbm.at[:, columns], rot.at[:, columns], rot_sem.at[c])

    def src_copy(k, i):
        return remote(
            src.at[k, peers[i]], rcv.at[k, ep], src_send.at[k, i], src_recv.at[k, i], hid, peers[i]
        )

    def x_copy(own, far, near, send, recv, half, i):
        first, to, target = (
            (0, right, far.at[0]),
            (1, left, far.at[1]),
            (3, right, near.at[0, pl.ds(half, half)]),
            (4, left, near.at[1, pl.ds(0, half)]),
            (2, right, near.at[0, pl.ds(0, half)]),
            (5, left, near.at[1, pl.ds(half, half)]),
        )[i]
        return remote(own.at[pl.ds(first * half, half)], target, send.at[i], recv.at[i], to, ep)

    def a_x(c, i):
        return x_copy(a_own[c], a_far[c], a_from[c], a_x_send.at[c], a_x_recv.at[c], 16, i)

    def b_x(n, i):
        return x_copy(
            b_own.at[n], b_far.at[n], b_from.at[n], b_x_send.at[n], b_x_recv.at[n], 32, i
        )

    def a_core(c):
        return remote(a_core_out[c], a_core_in[c], a_core_send.at[c], a_core_recv.at[c], other, ep)

    def b_core(n):
        return remote(
            b_core_out.at[n], b_core_in.at[n], b_core_send.at[n], b_core_recv.at[n], other, ep
        )

    def a_spread(c, i):
        return remote(
            a_sum[c].at[peers[i]], a_in[c].at[ep], a_in_send.at[c, i], a_in_recv.at[c, i],
            hid, peers[i],
        )

    def a_owner(c, i):
        return remote(
            a_pick[c].at[peers[i]], a_got[c].at[ep], a_own_send.at[c, i], a_own_recv.at[c, i],
            hid, peers[i],
        )

    def b_owner(n, i):
        return remote(
            b_pick.at[n, peers[i]], b_got.at[n, ep], b_own_send.at[n, i], b_own_recv.at[n, i],
            hid, peers[i],
        )

    def a_store(c):
        columns = pl.ds(A_STARTS[c], A_WIDTHS[c])
        return pltpu.make_async_copy(a_out[c], out_hbm.at[0, :, columns], a_out_sem.at[c])

    def b_store(n):
        columns = pl.ds(pl.multiple_of(n * B_WIDTH, B_WIDTH), B_WIDTH)
        return pltpu.make_async_copy(
            b_out.at[n], out_hbm.at[pl.ds(1, 2), :, columns], b_out_sem.at[n]
        )

    def sum_cores(own, core_in, half, start_x):
        own[0:2 * half] += core_in[0:2 * half]
        start_x(0)
        start_x(1)
        own[2 * half:6 * half] += core_in[2 * half:6 * half]
        start_x(2)
        start_x(3)
        own[6 * half:8 * half] += core_in[6 * half:8 * half]

    def pass_on(own, far, half, x_of):
        x_of(0).wait_recv()
        own[2 * half:3 * half] += far[0]
        x_of(4).start()
        x_of(1).wait_recv()
        own[5 * half:6 * half] += far[1]
        x_of(5).start()

    def total_of(own, near, half, rows, columns):
        return (
            own[6 * half + rows.start:6 * half + rows.stop, columns].astype(F32)
            + near[0, rows, columns].astype(F32)
            + near[1, rows, columns].astype(F32)
        ).astype(BF)

    def a_multiply(c):
        rot_copy(c).wait()

        @pl.loop(0, A_WIDTHS[c] // TILE)
        def _(t):
            here = pl.ds(pl.multiple_of(t * TILE, TILE), TILE)
            there = pl.ds(pl.multiple_of(A_STARTS[c] + t * TILE, TILE), TILE)
            total = dot(lhs_a[...], rot[:, there])
            a_core_out[c][:, here] = total[:128].astype(BF)
            a_own[c][:, here] = total[128:].astype(BF)

    def a_sum_cores(c):
        a_core(c).wait_recv()
        sum_cores(a_own[c], a_core_in[c], 16, lambda i: a_x(c, i).start())

    def a_pass_on(c):
        pass_on(a_own[c], a_far[c], 16, lambda i: a_x(c, i))

    def a_to_peers(c):
        for i in range(2, 6):
            a_x(c, i).wait_recv()
        eighth = A_WIDTHS[c] // 8
        for m in range(2):
            for q in range(8):
                a_sum[c][m * 8 + q] = total_of(
                    a_own[c], a_from[c], 16,
                    slice(m * 16, m * 16 + 16), slice(q * eighth, (q + 1) * eighth),
                )
        for i in range(OTHERS):
            a_spread(c, i).start()
        a_in[c][ep] = a_sum[c][ep]

    def a_to_owners(c):
        for i in range(OTHERS):
            a_spread(c, i).wait_recv()
        eighth = A_WIDTHS[c] // 8
        rows = dot(sel_a[...], a_in[c][...].reshape(256, eighth))
        a_pick[c][...] = rows.astype(BF).reshape(16, 32, eighth)
        for i in range(OTHERS):
            a_owner(c, i).start()
        a_got[c][ep] = a_pick[c][ep]

    def a_place(c):
        for i in range(OTHERS):
            a_owner(c, i).wait_recv()
        eighth = A_WIDTHS[c] // 8
        for q in range(8):
            both = jnp.concatenate([a_got[c][q], a_got[c][8 + q]], axis=0)
            a_out[c][:, q * eighth:(q + 1) * eighth] = dot(put_a[...], both).astype(BF)
        a_store(c).start()

    def b_multiply(n):
        here = pl.ds(pl.multiple_of(n * B_WIDTH, B_WIDTH), B_WIDTH)
        total = dot(lhs_b[...], rot[:, here])
        b_core_out[n] = total[:256].astype(BF)
        b_own[n] = total[256:].astype(BF)
        b_core(n).start()

    def b_sum_cores(n):
        b_core(n).wait_recv()
        sum_cores(b_own.at[n], b_core_in.at[n], 32, lambda i: b_x(n, i).start())

    def b_pass_on(n):
        pass_on(b_own.at[n], b_far.at[n], 32, lambda i: b_x(n, i))

    def b_to_owners(n):
        for i in range(2, 6):
            b_x(n, i).wait_recv()
        quarters = []
        for g in range(4):
            columns = slice(g * B_QUARTER, (g + 1) * B_QUARTER)
            quarters.append(jnp.concatenate([
                total_of(b_own.at[n], b_from.at[n], 32, slice(k * 32, k * 32 + 32), columns)
                for k in range(2)
            ], axis=1))
        rows = dot(sel_b[...], jnp.concatenate(quarters, axis=0))
        b_pick[n] = rows.astype(BF).reshape(16, 16, 2 * B_QUARTER)
        for i in range(OTHERS):
            b_owner(n, i).start()
        b_got[n, ep] = b_pick[n, ep]

    def b_place(n):
        for i in range(OTHERS):
            b_owner(n, i).wait_recv()
        rows = dot(put_b[...], b_got[n].reshape(256, 2 * B_QUARTER)).astype(BF)
        for k in range(2):
            for g in range(4):
                b_out[n, k, :, g * B_QUARTER:(g + 1) * B_QUARTER] = rows[
                    g * 64:(g + 1) * 64, k * B_QUARTER:(k + 1) * B_QUARTER
                ]
        b_store(n).start()

    for c in range(A_CHUNKS):
        rot_copy(c).start()

    r, s = iotas(256, 128)
    block = ((x + ring_offset((r // 32) % 4)) % 4) * 2 + jnp.where(r < 128, 1 - core, core)
    column = block * 16 + r % 16
    expert = (r // 16) % 2
    rows = sum(dot_t(onehot((expert == m) & (s == column)), gate_ref[m]) for m in range(2))
    lhs_a[...] = rows.astype(BF)

    column = (r % 8) * 16 + r // 16
    expert = (r // 8) % 2
    spread = [onehot((expert == m) & (s == column)) for m in range(2)]
    rows = sum(dot_t(spread[m], up_ref[m]) for m in range(2))
    src[0] = rows.astype(BF).reshape(16, 16, PIECE)
    rows = sum(dot(spread[m], down_ref[m]) for m in range(2))
    src[1] = rows.astype(BF).reshape(16, 16, PIECE)
    for k in range(2):
        rcv[k, ep] = src[k, ep]

    for c in range(A_CHUNKS):
        a_multiply(c)

    low, high, mine = ranges(hid, ep, placement_ref, count_ref)
    sel_a[...] = select_a(ep, low, high)
    put_a[...] = place_a(mine)
    sel_b[...] = select_b(low, high)
    r, s = iotas(256, 256)
    put_b[...] = onehot(s == (r % 16) * 16 + ((r // 16) % 4) * 4 + r // 64)
    r, s = iotas(512, 512)
    block = ((x + ring_offset((r // 64) % 4)) % 4) * 2 + jnp.where(r < 256, 1 - core, core)
    arrange[...] = onehot(
        s == ((r // 32) % 2) * 256 + (r % 16) * 16 + ((r // 16) % 2) * 8 + block
    )

    pl.semaphore_wait(barrier, 3 + OTHERS)

    for c in range(A_CHUNKS):
        a_core(c).start()
    for i in range(OTHERS):
        src_copy(0, i).start()
    a_sum_cores(0)
    for i in range(OTHERS):
        src_copy(1, i).start()
    a_sum_cores(1)
    a_pass_on(0)
    a_sum_cores(2)
    a_pass_on(1)
    a_to_peers(0)
    a_pass_on(2)

    for k in range(2):
        for i in range(OTHERS):
            src_copy(k, i).wait_recv()
    lhs_b[...] = dot(arrange[...], rcv[...].reshape(512, PIECE)).astype(BF)
    b_multiply(0)
    a_to_peers(1)

    stages = ((b_sum_cores, 0), (b_multiply, -1), (b_pass_on, 1), (b_to_owners, 2), (b_place, 3))
    extras = {
        0: (lambda: a_to_owners(0), lambda: a_to_peers(2)),
        1: (lambda: a_to_owners(1),),
        2: (lambda: a_to_owners(2), lambda: a_place(0), lambda: a_place(1)),
        3: (lambda: a_place(2),),
    }

    @pl.loop(0, B_CHUNKS + 3)
    def _(t):
        for stage, lag in stages:
            @pl.when((t >= lag) & (t < B_CHUNKS + lag))
            def _():
                stage(t - lag)
        for at, work in extras.items():
            @pl.when(t == at)
            def _():
                for one in work:
                    one()

    for k in range(2):
        for i in range(OTHERS):
            src_copy(k, i).wait_send()
    for c in range(A_CHUNKS):
        a_core(c).wait_send()
        for i in range(6):
            a_x(c, i).wait_send()
        for i in range(OTHERS):
            a_spread(c, i).wait_send()
            a_owner(c, i).wait_send()
        a_store(c).wait()

    @pl.loop(0, B_CHUNKS)
    def _(n):
        b_core(n).wait_send()
        for i in range(6):
            b_x(n, i).wait_send()
        for i in range(OTHERS):
            b_owner(n, i).wait_send()
        b_store(n).wait()


def on_device(gate_proj, up_proj, down_proj, rotation, placement, row_count):
    dma = pltpu.SemaphoreType.DMA
    vmem = pl.BlockSpec(memory_space=pltpu.VMEM)
    smem = pl.BlockSpec(memory_space=pltpu.SMEM)
    hbm = pl.BlockSpec(memory_space=pl.ANY)

    def held(*shape):
        return pltpu.VMEM(shape, BF)

    def per_a(shape_of):
        return [held(*shape_of(w)) for w in A_WIDTHS]

    b = B_CHUNKS
    scratch = [
        held(PIECE, HIDDEN), held(256, PIECE), held(512, PIECE),
        held(2, 16, 16, PIECE), held(2, 16, 16, PIECE),
        held(512, 256), held(64, 64), held(256, 128), held(256, 256), held(512, 512),
        *per_a(lambda w: (128, w)),
        *per_a(lambda w: (128, w)),
        *per_a(lambda w: (128, w)),
        *per_a(lambda w: (2, 16, w)),
        *per_a(lambda w: (2, 32, w)),
        *per_a(lambda w: (16, 16, w // 8)),
        *per_a(lambda w: (16, 16, w // 8)),
        *per_a(lambda w: (16, 32, w // 8)),
        *per_a(lambda w: (16, 32, w // 8)),
        *per_a(lambda w: (64, w)),
        held(b, 256, B_WIDTH), held(b, 256, B_WIDTH), held(b, 256, B_WIDTH),
        held(b, 2, 32, B_WIDTH), held(b, 2, 64, B_WIDTH),
        held(b, 16, 16, 2 * B_QUARTER), held(b, 16, 16, 2 * B_QUARTER),
        held(b, 2, 64, B_WIDTH),
        dma((A_CHUNKS,)), dma((2, OTHERS)), dma((2, OTHERS)),
        dma((A_CHUNKS,)), dma((A_CHUNKS,)), dma((A_CHUNKS, 6)), dma((A_CHUNKS, 6)),
        dma((A_CHUNKS, OTHERS)), dma((A_CHUNKS, OTHERS)),
        dma((A_CHUNKS, OTHERS)), dma((A_CHUNKS, OTHERS)), dma((A_CHUNKS,)),
        dma((b,)), dma((b,)), dma((b, 6)), dma((b, 6)),
        dma((b, OTHERS)), dma((b, OTHERS)), dma((b,)),
    ]
    out = pl.pallas_call(
        kernel,
        out_shape=jax.ShapeDtypeStruct((3, 64, HIDDEN), BF),
        in_specs=[smem, smem, vmem, vmem, vmem, hbm],
        out_specs=hbm,
        scratch_shapes=scratch,
        compiler_params=pltpu.CompilerParams(
            collective_id=0, has_side_effects=True, vmem_limit_bytes=60 * 1024 * 1024
        ),
        name="rotate_and_place",
    )(placement, row_count, gate_proj, up_proj, down_proj, rotation)
    return jnp.transpose(out, (1, 0, 2))[None]


def solution(mesh):
    in_specs = (
        P(None, "hid", "ep"),
        P(None, "hid", "ep"),
        P(None, "ep", "hid"),
        P("hid", None),
        P(),
        P(),
    )
    out_specs = P("ep", "hid", None, None)
    return jax.shard_map(
        on_device, mesh=mesh, in_specs=in_specs, out_specs=out_specs, check_vma=False
    )
```

```python
import jax
import jax.numpy as jnp
from jax import lax
from jax.experimental import pallas as pl
from jax.experimental.pallas import tpu as pltpu
from jax.sharding import PartitionSpec as P

MESH = pl.DeviceIdType.MESH
BF = jnp.bfloat16
F32 = jnp.float32
PEERS = (
    (0, 1), (0, 3), (1, 0), (3, 0), (1, 1), (3, 3), (1, 3), (3, 1),
    (0, 2), (2, 0), (1, 2), (2, 1), (3, 2), (2, 3), (2, 2),
)
OTHERS = len(PEERS)
HIDDEN = 7168
PIECE = 896
A_WIDTHS = (1024, 2048, 4096)
A_STARTS = (0, 1024, 3072)
A_CHUNKS = len(A_WIDTHS)
B_WIDTH = 1024
B_CHUNKS = HIDDEN // B_WIDTH
B_QUARTER = B_WIDTH // 4
TILE = 1024


def iotas(rows, cols):
    return (
        lax.broadcasted_iota(jnp.int32, (rows, cols), 0),
        lax.broadcasted_iota(jnp.int32, (rows, cols), 1),
    )


def onehot(condition):
    return jnp.where(condition, 1.0, 0.0).astype(BF)


def dot(a, b):
    return jnp.dot(a, b, preferred_element_type=F32)


def dot_t(a, b):
    return lax.dot_general(a, b, (((1,), (1,)), ((), ())), preferred_element_type=F32)


def ring_offset(index):
    return jnp.where(index == 0, 2, jnp.where(index == 1, 1, jnp.where(index == 2, 3, 0)))


def ranges(h, ep, placement_ref, count_ref):
    owners, _ = iotas(16, 256)
    low, high, mine = [], [], []
    for m in range(2):
        start = jnp.int32(0)
        count = jnp.int32(0)
        lo = jnp.zeros((16, 256), jnp.int32)
        hi = jnp.zeros((16, 256), jnp.int32)
        for t in range(16):
            o = placement_ref[m, t]
            end = start + lax.shift_right_logical(count_ref[m, o], 4)
            first = lax.shift_right_logical(start + 7 - h, 3)
            last = lax.shift_right_logical(end + 7 - h, 3)
            lo = jnp.where(owners == o, first, lo)
            hi = jnp.where(owners == o, last, hi)
            count = jnp.where(o == ep, last - first, count)
            start = end
        low.append(lo)
        high.append(hi)
        mine.append(count)
    return low, high, mine


def select_a(ep, low, high):
    first = ep < 8
    lo = jnp.where(first, low[0], low[1])
    hi = jnp.where(first, high[0], high[1])
    _, col = iotas(16, 256)
    e = col // 16
    place = jnp.where((lo <= e) & (e < hi), e - lo, -1)
    place = jnp.broadcast_to(place[:, None, :], (16, 32, 256)).reshape(512, 256)
    r, s = iotas(512, 256)
    return onehot((place == (r // 16) % 2) & (r % 16 == s % 16))


def place_a(mine):
    r, s = iotas(64, 64)
    slot = (s // 16) % 2 + jnp.where(s < 32, 0, mine[0])
    return onehot((slot == r // 16) & (r % 16 == s % 16))


def select_b(low, high):
    _, col = iotas(16, 128)
    m = (col // 16) % 2
    e = col % 16
    low = [v[:, :128] for v in low]
    high = [v[:, :128] for v in high]
    lo = jnp.where(m == 0, low[0], low[1])
    hi = jnp.where(m == 0, high[0], high[1])
    slot = e - lo + jnp.where(m == 0, 0, high[0] - low[0])
    slot = jnp.where((lo <= e) & (e < hi), slot, -1)
    slot = jnp.broadcast_to(slot[:, None, :], (16, 16, 128)).reshape(256, 128)
    r, s = iotas(256, 128)
    return onehot((slot == (r // 4) % 4) & (r % 4 == s // 32))


def kernel(
    placement_ref, count_ref, gate_ref, up_ref, down_ref, rot_hbm, *scratch
):
    scratch = list(scratch)

    def take(count):
        taken = scratch[:count]
        del scratch[:count]
        return taken

    a_got = take(A_CHUNKS)
    b_got, put_hbm = take(2)
    rot, lhs_a, lhs_b, src, rcv, sel_a, put_a, sel_b, arrange = take(9)
    a_core_out, a_core_in, a_own, a_far, a_near, a_sum, a_in, a_pick = (
        take(A_CHUNKS) for _ in range(8)
    )
    b_core_out, b_core_in, b_own, b_far, b_near, b_pick = take(6)
    rot_sem, put_sem, src_send, src_recv = take(4)
    a_core_send, a_core_recv, a_x_send, a_far_recv, a_near_recv = take(5)
    a_in_send, a_in_recv, a_own_send, a_own_recv, a_self = take(5)
    b_core_send, b_core_recv, b_x_send, b_far_recv, b_near_recv = take(5)
    b_own_send, b_own_recv, b_self = take(3)

    hid = lax.axis_index("hid")
    ep = lax.axis_index("ep")
    x, core = hid // 2, hid % 2
    z, y = ep // 4, ep % 4
    right = lax.rem(x + 1, 4) * 2 + core
    left = lax.rem(x + 3, 4) * 2 + core
    other = x * 2 + 1 - core
    peers = [lax.rem(z + dz, 4) * 4 + lax.rem(y + dy, 4) for dz, dy in PEERS]

    def remote(source, target, send, recv, h, e):
        return pltpu.make_async_remote_copy(
            source, target, send, recv, device_id=(h, e), device_id_type=MESH
        )

    def wait_bytes(ref, sem):
        pltpu.make_async_copy(ref, ref, sem).wait()

    barrier = pltpu.get_barrier_semaphore()
    for h in (right, left, other):
        pl.semaphore_signal(barrier, 1, device_id=(h, ep), device_id_type=MESH)
    for p in peers:
        pl.semaphore_signal(barrier, 1, device_id=(hid, p), device_id_type=MESH)

    def rot_copy(c):
        columns = pl.ds(A_STARTS[c], A_WIDTHS[c])
        return pltpu.make_async_copy(rot_hbm.at[:, columns], rot.at[:, columns], rot_sem.at[c])

    def src_copy(k, i):
        return remote(
            src.at[k, peers[i]], rcv.at[k, ep], src_send, src_recv, hid, peers[i]
        )

    def x_copy(own, far, near, send, far_recv, near_recv, half, i):
        first, to, target, recv = (
            (0, right, far.at[0], far_recv),
            (1, left, far.at[1], far_recv),
            (3, right, near.at[0, pl.ds(half, half)], near_recv),
            (4, left, near.at[1, pl.ds(0, half)], near_recv),
            (2, right, near.at[0, pl.ds(0, half)], near_recv),
            (5, left, near.at[1, pl.ds(half, half)], near_recv),
        )[i]
        return remote(own.at[pl.ds(first * half, half)], target, send, recv, to, ep)

    def a_x(c, i):
        return x_copy(
            a_own[c], a_far[c], a_near[c],
            a_x_send.at[c], a_far_recv.at[c], a_near_recv.at[c], 16, i,
        )

    def b_x(n, i):
        return x_copy(
            b_own.at[n], b_far.at[n], b_near.at[n],
            b_x_send, b_far_recv.at[n], b_near_recv.at[n], 32, i,
        )

    def a_core(c):
        return remote(a_core_out[c], a_core_in[c], a_core_send.at[c], a_core_recv.at[c], other, ep)

    def b_core(n):
        return remote(
            b_core_out.at[n], b_core_in.at[n], b_core_send, b_core_recv.at[n], other, ep
        )

    def a_spread(c, i):
        return remote(
            a_sum[c].at[peers[i]], a_in[c].at[ep], a_in_send.at[c], a_in_recv.at[c], hid, peers[i]
        )

    def a_owner(c, i):
        return remote(
            a_pick[c].at[peers[i]], a_got[c].at[ep], a_own_send.at[c], a_own_recv.at[c],
            hid, peers[i],
        )

    def a_keep(c):
        return pltpu.make_async_copy(a_pick[c].at[ep], a_got[c].at[ep], a_self.at[c])

    def b_owner(n, i):
        return remote(
            b_pick.at[n, peers[i]], b_got.at[n, ep], b_own_send, b_own_recv, hid, peers[i]
        )

    def b_keep(n):
        return pltpu.make_async_copy(b_pick.at[n, ep], b_got.at[n, ep], b_self)

    put_copy = pltpu.make_async_copy(put_a, put_hbm, put_sem)

    def sum_cores(own, core_in, half, start_x):
        own[0:2 * half] += core_in[0:2 * half]
        start_x(0)
        start_x(1)
        own[2 * half:6 * half] += core_in[2 * half:6 * half]
        start_x(2)
        start_x(3)
        own[6 * half:8 * half] += core_in[6 * half:8 * half]

    def pass_on(own, far, far_recv, half, x_of):
        wait_bytes(far, far_recv)
        own[2 * half:3 * half] += far[0]
        x_of(4).start()
        own[5 * half:6 * half] += far[1]
        x_of(5).start()

    def total_of(own, near, half, rows, columns):
        return (
            own[6 * half + rows.start:6 * half + rows.stop, columns].astype(F32)
            + near[0, rows, columns].astype(F32)
            + near[1, rows, columns].astype(F32)
        ).astype(BF)

    def a_multiply(c):
        rot_copy(c).wait()

        @pl.loop(0, A_WIDTHS[c] // TILE)
        def _(t):
            here = pl.ds(pl.multiple_of(t * TILE, TILE), TILE)
            there = pl.ds(pl.multiple_of(A_STARTS[c] + t * TILE, TILE), TILE)
            total = dot(lhs_a[...], rot[:, there])
            a_core_out[c][:, here] = total[:128].astype(BF)
            a_own[c][:, here] = total[128:].astype(BF)

    def a_sum_cores(c):
        a_core(c).wait_recv()
        sum_cores(a_own[c], a_core_in[c], 16, lambda i: a_x(c, i).start())

    def a_pass_on(c):
        pass_on(a_own[c], a_far[c], a_far_recv.at[c], 16, lambda i: a_x(c, i))

    def a_to_peers(c):
        wait_bytes(a_near[c], a_near_recv.at[c])
        eighth = A_WIDTHS[c] // 8
        for m in range(2):
            for q in range(8):
                a_sum[c][m * 8 + q] = total_of(
                    a_own[c], a_near[c], 16,
                    slice(m * 16, m * 16 + 16), slice(q * eighth, (q + 1) * eighth),
                )
        for i in range(OTHERS):
            a_spread(c, i).start()
        a_in[c][ep] = a_sum[c][ep]

    def a_to_owners(c):
        wait_bytes(a_in[c].at[pl.ds(0, OTHERS)], a_in_recv.at[c])
        eighth = A_WIDTHS[c] // 8
        rows = dot(sel_a[...], a_in[c][...].reshape(256, eighth))
        a_pick[c][...] = rows.astype(BF).reshape(16, 32, eighth)
        for i in range(OTHERS):
            a_owner(c, i).start()
        a_keep(c).start()

    def b_multiply(n):
        here = pl.ds(pl.multiple_of(n * B_WIDTH, B_WIDTH), B_WIDTH)
        total = dot(lhs_b[...], rot[:, here])
        b_core_out[n] = total[:256].astype(BF)
        b_own[n] = total[256:].astype(BF)
        b_core(n).start()

    def b_sum_cores(n):
        b_core(n).wait_recv()
        sum_cores(b_own.at[n], b_core_in.at[n], 32, lambda i: b_x(n, i).start())

    def b_pass_on(n):
        pass_on(b_own.at[n], b_far.at[n], b_far_recv.at[n], 32, lambda i: b_x(n, i))

    def b_to_owners(n):
        wait_bytes(b_near.at[n], b_near_recv.at[n])
        quarters = []
        for g in range(4):
            columns = slice(g * B_QUARTER, (g + 1) * B_QUARTER)
            quarters.append(jnp.concatenate([
                total_of(b_own.at[n], b_near.at[n], 32, slice(k * 32, k * 32 + 32), columns)
                for k in range(2)
            ], axis=1))
        rows = dot(sel_b[...], jnp.concatenate(quarters, axis=0))
        b_pick[n] = rows.astype(BF).reshape(16, 16, 2 * B_QUARTER)
        for i in range(OTHERS):
            b_owner(n, i).start()
        b_keep(n).start()

    for c in range(A_CHUNKS):
        rot_copy(c).start()

    r, s = iotas(256, 128)
    block = ((x + ring_offset((r // 32) % 4)) % 4) * 2 + jnp.where(r < 128, 1 - core, core)
    column = block * 16 + r % 16
    expert = (r // 16) % 2
    rows = sum(dot_t(onehot((expert == m) & (s == column)), gate_ref[m]) for m in range(2))
    lhs_a[...] = rows.astype(BF)

    column = (r % 8) * 16 + r // 16
    expert = (r // 8) % 2
    spread = [onehot((expert == m) & (s == column)) for m in range(2)]
    rows = sum(dot_t(spread[m], up_ref[m]) for m in range(2))
    src[0] = rows.astype(BF).reshape(16, 16, PIECE)
    rows = sum(dot(spread[m], down_ref[m]) for m in range(2))
    src[1] = rows.astype(BF).reshape(16, 16, PIECE)
    for k in range(2):
        rcv[k, ep] = src[k, ep]

    for c in range(A_CHUNKS):
        a_multiply(c)

    low, high, mine = ranges(hid, ep, placement_ref, count_ref)
    sel_a[...] = select_a(ep, low, high)
    put_a[...] = place_a(mine)
    put_copy.start()
    sel_b[...] = select_b(low, high)
    r, s = iotas(512, 512)
    block = ((x + ring_offset((r // 64) % 4)) % 4) * 2 + jnp.where(r < 256, 1 - core, core)
    arrange[...] = onehot(
        s == ((r // 32) % 2) * 256 + (r % 16) * 16 + ((r // 16) % 2) * 8 + block
    )

    pl.semaphore_wait(barrier, 3 + OTHERS)

    for c in range(A_CHUNKS):
        a_core(c).start()
    for i in range(OTHERS):
        src_copy(0, i).start()
    a_sum_cores(0)
    for i in range(OTHERS):
        src_copy(1, i).start()
    a_sum_cores(1)
    a_pass_on(0)
    a_sum_cores(2)
    a_pass_on(1)
    a_to_peers(0)
    a_pass_on(2)

    wait_bytes(rcv.at[:, pl.ds(0, OTHERS)], src_recv)
    lhs_b[...] = dot(arrange[...], rcv[...].reshape(512, PIECE)).astype(BF)
    b_multiply(0)
    a_to_peers(1)

    stages = ((b_sum_cores, 0), (b_multiply, -1), (b_pass_on, 1), (b_to_owners, 2))
    extras = {
        0: (lambda: a_to_owners(0), lambda: a_to_peers(2)),
        1: (lambda: a_to_owners(1),),
        2: (lambda: a_to_owners(2),),
    }

    @pl.loop(0, B_CHUNKS + 2)
    def _(t):
        for stage, lag in stages:
            @pl.when((t >= lag) & (t < B_CHUNKS + lag))
            def _():
                stage(t - lag)
        for at, work in extras.items():
            @pl.when(t == at)
            def _():
                for one in work:
                    one()

    rest = pl.ds(0, OTHERS)
    put_copy.wait()
    wait_bytes(src.at[:, rest], src_send)
    for c in range(A_CHUNKS):
        a_core(c).wait_send()
        wait_bytes(a_own[c].at[pl.ds(0, 96)], a_x_send.at[c])
        wait_bytes(a_sum[c].at[rest], a_in_send.at[c])
        wait_bytes(a_pick[c].at[rest], a_own_send.at[c])
        a_keep(c).wait()
        wait_bytes(a_got[c].at[rest], a_own_recv.at[c])
    wait_bytes(b_core_out, b_core_send)
    wait_bytes(b_own.at[:, pl.ds(0, 192)], b_x_send)
    wait_bytes(b_pick.at[:, rest], b_own_send)
    wait_bytes(b_pick.at[:, 0], b_self)
    wait_bytes(b_got.at[:, rest], b_own_recv)


def place_kernel(*refs):
    a_got, (b_got, put_hbm, out_hbm) = refs[:A_CHUNKS], refs[A_CHUNKS:A_CHUNKS + 3]
    a_in, (b_in, put_a) = refs[A_CHUNKS + 3:2 * A_CHUNKS + 3], refs[2 * A_CHUNKS + 3:2 * A_CHUNKS + 5]
    a_out, b_out, a_load, b_load, put_load, a_sem, b_sem = refs[2 * A_CHUNKS + 5:]

    def a_read(c):
        return pltpu.make_async_copy(a_got[c], a_in[c], a_load.at[c])

    def b_read(n):
        return pltpu.make_async_copy(b_got.at[n], b_in.at[n], b_load.at[n])

    def a_store(c):
        columns = pl.ds(A_STARTS[c], A_WIDTHS[c])
        return pltpu.make_async_copy(a_out.at[:, columns], out_hbm.at[0, :, columns], a_sem.at[c])

    def b_store(n):
        columns = pl.ds(pl.multiple_of(n * B_WIDTH, B_WIDTH), B_WIDTH)
        return pltpu.make_async_copy(
            b_out.at[:, :, columns], out_hbm.at[pl.ds(1, 2), :, columns], b_sem.at[n]
        )

    put_copy = pltpu.make_async_copy(put_hbm, put_a, put_load)
    put_copy.start()
    for c in range(A_CHUNKS):
        a_read(c).start()
    for n in range(B_CHUNKS):
        b_read(n).start()
    r, s = iotas(256, 256)
    put_b = onehot(s == (r % 16) * 16 + ((r // 16) % 4) * 4 + r // 64)
    put_copy.wait()
    for c in range(A_CHUNKS):
        a_read(c).wait()
        eighth = A_WIDTHS[c] // 8
        for q in range(8):
            both = jnp.concatenate([a_in[c][q], a_in[c][8 + q]], axis=0)
            first = A_STARTS[c] + q * eighth
            a_out[:, first:first + eighth] = dot(put_a[...], both).astype(BF)
        a_store(c).start()
    for n in range(B_CHUNKS):
        b_read(n).wait()
        rows = dot(put_b, b_in[n].reshape(256, 2 * B_QUARTER)).astype(BF)
        for k in range(2):
            for g in range(4):
                first = n * B_WIDTH + g * B_QUARTER
                b_out[k, :, first:first + B_QUARTER] = rows[
                    g * 64:(g + 1) * 64, k * B_QUARTER:(k + 1) * B_QUARTER
                ]
        b_store(n).start()
    for c in range(A_CHUNKS):
        a_store(c).wait()
    for n in range(B_CHUNKS):
        b_store(n).wait()


def on_device(gate_proj, up_proj, down_proj, rotation, placement, row_count):
    dma = pltpu.SemaphoreType.DMA
    vmem = pl.BlockSpec(memory_space=pltpu.VMEM)
    smem = pl.BlockSpec(memory_space=pltpu.SMEM)
    hbm = pl.BlockSpec(memory_space=pl.ANY)

    def held(*shape):
        return pltpu.VMEM(shape, BF)

    def per_a(shape_of):
        return [held(*shape_of(w)) for w in A_WIDTHS]

    b = B_CHUNKS
    scratch = [
        held(PIECE, HIDDEN), held(256, PIECE), held(512, PIECE),
        held(2, 16, 16, PIECE), held(2, 16, 16, PIECE),
        held(512, 256), held(64, 64), held(256, 128), held(512, 512),
        *per_a(lambda w: (128, w)),
        *per_a(lambda w: (128, w)),
        *per_a(lambda w: (128, w)),
        *per_a(lambda w: (2, 16, w)),
        *per_a(lambda w: (2, 32, w)),
        *per_a(lambda w: (16, 16, w // 8)),
        *per_a(lambda w: (16, 16, w // 8)),
        *per_a(lambda w: (16, 32, w // 8)),
        held(b, 256, B_WIDTH), held(b, 256, B_WIDTH), held(b, 256, B_WIDTH),
        held(b, 2, 32, B_WIDTH), held(b, 2, 64, B_WIDTH),
        held(b, 16, 16, 2 * B_QUARTER),
        dma((A_CHUNKS,)), dma, dma, dma,
        dma((A_CHUNKS,)), dma((A_CHUNKS,)), dma((A_CHUNKS,)), dma((A_CHUNKS,)), dma((A_CHUNKS,)),
        dma((A_CHUNKS,)), dma((A_CHUNKS,)), dma((A_CHUNKS,)), dma((A_CHUNKS,)), dma((A_CHUNKS,)),
        dma, dma((b,)), dma, dma((b,)), dma((b,)),
        dma, dma, dma,
    ]
    arrived = [
        *(jax.ShapeDtypeStruct((16, 32, w // 8), BF) for w in A_WIDTHS),
        jax.ShapeDtypeStruct((b, 16, 16, 2 * B_QUARTER), BF),
        jax.ShapeDtypeStruct((64, 64), BF),
    ]
    limit = 60 * 1024 * 1024
    got = pl.pallas_call(
        kernel,
        out_shape=arrived,
        in_specs=[smem, smem, vmem, vmem, vmem, hbm],
        out_specs=[hbm] * len(arrived),
        scratch_shapes=scratch,
        compiler_params=pltpu.CompilerParams(
            collective_id=0, has_side_effects=True, vmem_limit_bytes=limit
        ),
        name="rotate_and_send",
    )(placement, row_count, gate_proj, up_proj, down_proj, rotation)
    out = pl.pallas_call(
        place_kernel,
        out_shape=jax.ShapeDtypeStruct((3, 64, HIDDEN), BF),
        in_specs=[hbm] * len(got),
        out_specs=hbm,
        scratch_shapes=[
            *(held(*v.shape) for v in arrived),
            held(64, HIDDEN), held(2, 64, HIDDEN),
            dma((A_CHUNKS,)), dma((b,)), dma, dma((A_CHUNKS,)), dma((b,)),
        ],
        compiler_params=pltpu.CompilerParams(vmem_limit_bytes=limit),
        name="place",
    )(*got)
    return jnp.transpose(out, (1, 0, 2))[None]


def solution(mesh):
    in_specs = (
        P(None, "hid", "ep"),
        P(None, "hid", "ep"),
        P(None, "ep", "hid"),
        P("hid", None),
        P(),
        P(),
    )
    out_specs = P("ep", "hid", None, None)
    return jax.shard_map(
        on_device, mesh=mesh, in_specs=in_specs, out_specs=out_specs, check_vma=False
    )
```

```python
import jax
import jax.numpy as jnp
from jax import lax
from jax.experimental import pallas as pl
from jax.experimental.pallas import tpu as pltpu
from jax.sharding import PartitionSpec as P

MESH = pl.DeviceIdType.MESH
BF = jnp.bfloat16
F32 = jnp.float32
PEERS = (
    (0, 1), (0, 3), (1, 0), (3, 0), (1, 1), (3, 3), (1, 3), (3, 1),
    (0, 2), (2, 0), (1, 2), (2, 1), (3, 2), (2, 3), (2, 2),
)
OTHERS = len(PEERS)
HIDDEN = 7168
PIECE = 896
A_WIDTHS = (1024, 2048, 2048, 2048)
A_STARTS = (0, 1024, 3072, 5120)
A_CHUNKS = len(A_WIDTHS)
B_WIDTH = 1024
B_CHUNKS = 6
C_WIDTH = 512
C_START = B_CHUNKS * B_WIDTH
C_CHUNKS = (HIDDEN - C_START) // C_WIDTH
TILE = 1024


def iotas(rows, cols):
    return (
        lax.broadcasted_iota(jnp.int32, (rows, cols), 0),
        lax.broadcasted_iota(jnp.int32, (rows, cols), 1),
    )


def onehot(condition):
    return jnp.where(condition, 1.0, 0.0).astype(BF)


def dot(a, b):
    return jnp.dot(a, b, preferred_element_type=F32)


def dot_t(a, b):
    return lax.dot_general(a, b, (((1,), (1,)), ((), ())), preferred_element_type=F32)


def ring_offset(index):
    return jnp.where(index == 0, 2, jnp.where(index == 1, 1, jnp.where(index == 2, 3, 0)))


def ranges(h, ep, placement_ref, count_ref):
    owners, _ = iotas(16, 256)
    low, high, mine = [], [], []
    for m in range(2):
        start = jnp.int32(0)
        count = jnp.int32(0)
        lo = jnp.zeros((16, 256), jnp.int32)
        hi = jnp.zeros((16, 256), jnp.int32)
        for t in range(16):
            o = placement_ref[m, t]
            end = start + lax.shift_right_logical(count_ref[m, o], 4)
            first = lax.shift_right_logical(start + 7 - h, 3)
            last = lax.shift_right_logical(end + 7 - h, 3)
            lo = jnp.where(owners == o, first, lo)
            hi = jnp.where(owners == o, last, hi)
            count = jnp.where(o == ep, last - first, count)
            start = end
        low.append(lo)
        high.append(hi)
        mine.append(count)
    return low, high, mine


def select_a(ep, low, high):
    first = ep < 8
    lo = jnp.where(first, low[0], low[1])
    hi = jnp.where(first, high[0], high[1])
    _, col = iotas(16, 256)
    e = col // 16
    place = jnp.where((lo <= e) & (e < hi), e - lo, -1)
    place = jnp.broadcast_to(place[:, None, :], (16, 32, 256)).reshape(512, 256)
    r, s = iotas(512, 256)
    return onehot((place == (r // 16) % 2) & (r % 16 == s % 16))


def place_a(mine):
    r, s = iotas(64, 64)
    slot = (s // 16) % 2 + jnp.where(s < 32, 0, mine[0])
    return onehot((slot == r // 16) & (r % 16 == s % 16))


def select_b(low, high):
    _, col = iotas(16, 128)
    m = (col // 16) % 2
    e = col % 16
    low = [v[:, :128] for v in low]
    high = [v[:, :128] for v in high]
    lo = jnp.where(m == 0, low[0], low[1])
    hi = jnp.where(m == 0, high[0], high[1])
    slot = e - lo + jnp.where(m == 0, 0, high[0] - low[0])
    slot = jnp.where((lo <= e) & (e < hi), slot, -1)
    slot = jnp.broadcast_to(slot[:, None, :], (16, 16, 128)).reshape(256, 128)
    r, s = iotas(256, 128)
    return onehot((slot == (r // 4) % 4) & (r % 4 == s // 32))


def kernel(
    placement_ref, count_ref, gate_hbm, up_hbm, down_hbm, rot_hbm, *scratch
):
    scratch = list(scratch)

    def take(count):
        taken = scratch[:count]
        del scratch[:count]
        return taken

    a_got = take(A_CHUNKS)
    b_got, *c_got = take(1 + C_CHUNKS)
    (put_hbm,) = take(1)
    gate, up, down = take(3)
    rot, lhs_a, lhs_b, src, rcv, sel_a, put_a, sel_b, arrange = take(9)
    a_core_out, a_core_in, a_own, a_far, a_near, a_sum, a_in, a_pick = (
        take(A_CHUNKS) for _ in range(8)
    )
    b_core_out, b_core_in, b_own, b_far, b_near, b_pick = take(6)
    c_core_out, c_core_in, c_own, c_far, c_near, c_pick = (take(C_CHUNKS) for _ in range(6))
    in_sem, rot_sem, put_sem, src_send, src_recv = take(5)
    a_core_send, a_core_recv, a_x_send, a_far_recv, a_near_recv = take(5)
    a_in_send, a_in_recv, a_own_send, a_own_recv, a_self = take(5)
    b_core_send, b_core_recv, b_x_send, b_far_recv, b_near_recv = take(5)
    b_own_send, b_own_recv, b_self = take(3)
    c_core_send, c_core_recv, c_x_send, c_far_recv, c_near_recv = take(5)
    c_own_send, c_own_recv, c_self = take(3)

    hid = lax.axis_index("hid")
    ep = lax.axis_index("ep")
    x, core = hid // 2, hid % 2
    z, y = ep // 4, ep % 4
    right = lax.rem(x + 1, 4) * 2 + core
    left = lax.rem(x + 3, 4) * 2 + core
    other = x * 2 + 1 - core
    peers = [lax.rem(z + dz, 4) * 4 + lax.rem(y + dy, 4) for dz, dy in PEERS]

    def remote(source, target, send, recv, h, e):
        return pltpu.make_async_remote_copy(
            source, target, send, recv, device_id=(h, e), device_id_type=MESH
        )

    def wait_bytes(ref, sem):
        pltpu.make_async_copy(ref, ref, sem).wait()

    barrier = pltpu.get_barrier_semaphore()
    for h in (right, left, other):
        pl.semaphore_signal(barrier, 1, device_id=(h, ep), device_id_type=MESH)
    for p in peers:
        pl.semaphore_signal(barrier, 1, device_id=(hid, p), device_id_type=MESH)

    def rot_copy(c):
        columns = pl.ds(A_STARTS[c], A_WIDTHS[c])
        return pltpu.make_async_copy(rot_hbm.at[:, columns], rot.at[:, columns], rot_sem.at[c])

    def src_copy(i):
        return remote(
            src.at[peers[i]], rcv.at[ep], src_send, src_recv, hid, peers[i]
        )

    def x_copy(own, far, near, send, far_recv, near_recv, half, i):
        first, to, target, recv = (
            (0, right, far.at[0], far_recv),
            (1, left, far.at[1], far_recv),
            (3, right, near.at[0, pl.ds(half, half)], near_recv),
            (4, left, near.at[1, pl.ds(0, half)], near_recv),
            (2, right, near.at[0, pl.ds(0, half)], near_recv),
            (5, left, near.at[1, pl.ds(half, half)], near_recv),
        )[i]
        return remote(own.at[pl.ds(first * half, half)], target, send, recv, to, ep)

    def a_x(c, i):
        return x_copy(
            a_own[c], a_far[c], a_near[c],
            a_x_send.at[c], a_far_recv.at[c], a_near_recv.at[c], 16, i,
        )

    def b_x(n, i):
        return x_copy(
            b_own.at[n], b_far.at[n], b_near.at[n],
            b_x_send, b_far_recv.at[n], b_near_recv.at[n], 32, i,
        )

    def c_x(n, i):
        return x_copy(
            c_own[n], c_far[n], c_near[n],
            c_x_send.at[n], c_far_recv.at[n], c_near_recv.at[n], 32, i,
        )

    def c_core(n):
        return remote(c_core_out[n], c_core_in[n], c_core_send.at[n], c_core_recv.at[n], other, ep)

    def c_owner(n, i):
        return remote(
            c_pick[n].at[peers[i]], c_got[n].at[ep], c_own_send.at[n], c_own_recv.at[n],
            hid, peers[i],
        )

    def c_keep(n):
        return pltpu.make_async_copy(c_pick[n].at[ep], c_got[n].at[ep], c_self.at[n])

    def a_core(c):
        return remote(a_core_out[c], a_core_in[c], a_core_send.at[c], a_core_recv.at[c], other, ep)

    def b_core(n):
        return remote(
            b_core_out.at[n], b_core_in.at[n], b_core_send, b_core_recv.at[n], other, ep
        )

    def a_spread(c, i):
        return remote(
            a_sum[c].at[peers[i]], a_in[c].at[ep], a_in_send.at[c], a_in_recv.at[c], hid, peers[i]
        )

    def a_owner(c, i):
        return remote(
            a_pick[c].at[peers[i]], a_got[c].at[ep], a_own_send.at[c], a_own_recv.at[c],
            hid, peers[i],
        )

    def a_keep(c):
        return pltpu.make_async_copy(a_pick[c].at[ep], a_got[c].at[ep], a_self.at[c])

    def b_owner(n, i):
        return remote(
            b_pick.at[n, peers[i]], b_got.at[n, ep], b_own_send, b_own_recv, hid, peers[i]
        )

    def b_keep(n):
        return pltpu.make_async_copy(b_pick.at[n, ep], b_got.at[n, ep], b_self)

    put_copy = pltpu.make_async_copy(put_a, put_hbm, put_sem)
    in_copies = [
        pltpu.make_async_copy(source, target, in_sem.at[i])
        for i, (source, target) in enumerate(((gate_hbm, gate), (up_hbm, up), (down_hbm, down)))
    ]

    def sum_cores(own, core_in, half, start_x):
        own[0:2 * half] += core_in[0:2 * half]
        start_x(0)
        start_x(1)
        own[2 * half:6 * half] += core_in[2 * half:6 * half]
        start_x(2)
        start_x(3)
        own[6 * half:8 * half] += core_in[6 * half:8 * half]

    def pass_on(own, far, far_recv, half, x_of):
        wait_bytes(far, far_recv)
        own[2 * half:3 * half] += far[0]
        x_of(4).start()
        own[5 * half:6 * half] += far[1]
        x_of(5).start()

    def total_of(own, near, half, rows, columns):
        return (
            own[6 * half + rows.start:6 * half + rows.stop, columns].astype(F32)
            + near[0, rows, columns].astype(F32)
            + near[1, rows, columns].astype(F32)
        ).astype(BF)

    def a_multiply(c):
        rot_copy(c).wait()

        @pl.loop(0, A_WIDTHS[c] // TILE)
        def _(t):
            here = pl.ds(pl.multiple_of(t * TILE, TILE), TILE)
            there = pl.ds(pl.multiple_of(A_STARTS[c] + t * TILE, TILE), TILE)
            total = dot(lhs_a[...], rot[:, there])
            a_core_out[c][:, here] = total[:128].astype(BF)
            a_own[c][:, here] = total[128:].astype(BF)

    def a_sum_cores(c):
        a_core(c).wait_recv()
        sum_cores(a_own[c], a_core_in[c], 16, lambda i: a_x(c, i).start())

    def a_pass_on(c):
        pass_on(a_own[c], a_far[c], a_far_recv.at[c], 16, lambda i: a_x(c, i))

    def a_to_peers(c):
        wait_bytes(a_near[c], a_near_recv.at[c])
        eighth = A_WIDTHS[c] // 8
        for m in range(2):
            for q in range(8):
                a_sum[c][m * 8 + q] = total_of(
                    a_own[c], a_near[c], 16,
                    slice(m * 16, m * 16 + 16), slice(q * eighth, (q + 1) * eighth),
                )
        for i in range(OTHERS):
            a_spread(c, i).start()
        a_in[c][ep] = a_sum[c][ep]

    def a_to_owners(c):
        wait_bytes(a_in[c].at[pl.ds(0, OTHERS)], a_in_recv.at[c])
        eighth = A_WIDTHS[c] // 8
        rows = dot(sel_a[...], a_in[c][...].reshape(256, eighth))
        a_pick[c][...] = rows.astype(BF).reshape(16, 32, eighth)
        for i in range(OTHERS):
            a_owner(c, i).start()
        a_keep(c).start()

    def multiply(width, start, core_out, own):
        total = dot(lhs_b[...], rot[:, pl.ds(start, width)])
        core_out[...] = total[:256].astype(BF)
        own[...] = total[256:].astype(BF)

    def pick_rows(width, own, near, pick):
        quarter = width // 4
        quarters = []
        for g in range(4):
            columns = slice(g * quarter, (g + 1) * quarter)
            quarters.append(jnp.concatenate([
                total_of(own, near, 32, slice(k * 32, k * 32 + 32), columns) for k in range(2)
            ], axis=1))
        rows = dot(sel_b[...], jnp.concatenate(quarters, axis=0))
        pick[...] = rows.astype(BF).reshape(16, 16, 2 * quarter)

    def b_multiply(n):
        start = pl.multiple_of(n * B_WIDTH, B_WIDTH)
        multiply(B_WIDTH, start, b_core_out.at[n], b_own.at[n])
        b_core(n).start()

    def b_sum_cores(n):
        b_core(n).wait_recv()
        sum_cores(b_own.at[n], b_core_in.at[n], 32, lambda i: b_x(n, i).start())

    def b_pass_on(n):
        pass_on(b_own.at[n], b_far.at[n], b_far_recv.at[n], 32, lambda i: b_x(n, i))

    def b_to_owners(n):
        wait_bytes(b_near.at[n], b_near_recv.at[n])
        pick_rows(B_WIDTH, b_own.at[n], b_near.at[n], b_pick.at[n])
        for i in range(OTHERS):
            b_owner(n, i).start()
        b_keep(n).start()

    def c_multiply(n):
        multiply(C_WIDTH, C_START + n * C_WIDTH, c_core_out[n], c_own[n])
        c_core(n).start()

    def c_sum_cores(n):
        c_core(n).wait_recv()
        sum_cores(c_own[n], c_core_in[n], 32, lambda i: c_x(n, i).start())

    def c_pass_on(n):
        pass_on(c_own[n], c_far[n], c_far_recv.at[n], 32, lambda i: c_x(n, i))

    def c_to_owners(n):
        wait_bytes(c_near[n], c_near_recv.at[n])
        pick_rows(C_WIDTH, c_own[n], c_near[n], c_pick[n])
        for i in range(OTHERS):
            c_owner(n, i).start()
        c_keep(n).start()

    for copy in in_copies:
        copy.start()
    for c in range(A_CHUNKS):
        rot_copy(c).start()

    r, s = iotas(256, 128)
    block = ((x + ring_offset((r // 32) % 4)) % 4) * 2 + jnp.where(r < 128, 1 - core, core)
    column = block * 16 + r % 16
    expert = (r // 16) % 2
    in_copies[0].wait()
    rows = sum(dot_t(onehot((expert == m) & (s == column)), gate[m]) for m in range(2))
    lhs_a[...] = rows.astype(BF)

    column = (r % 8) * 16 + r // 16
    expert = (r // 8) % 2
    spread = [onehot((expert == m) & (s == column)) for m in range(2)]
    in_copies[1].wait()
    rows = sum(dot_t(spread[m], up[m]) for m in range(2))
    src[:, 0] = rows.astype(BF).reshape(16, 16, PIECE)
    in_copies[2].wait()
    rows = sum(dot(spread[m], down[m]) for m in range(2))
    src[:, 1] = rows.astype(BF).reshape(16, 16, PIECE)
    a_multiply(0)

    pl.semaphore_wait(barrier, 3 + OTHERS)

    a_core(0).start()
    for i in range(OTHERS):
        src_copy(i).start()
    a_multiply(1)
    a_core(1).start()
    a_sum_cores(0)
    a_multiply(2)
    a_core(2).start()
    a_sum_cores(1)
    a_pass_on(0)
    a_multiply(3)
    a_core(3).start()
    a_sum_cores(2)
    a_pass_on(1)
    rcv[ep] = src[ep]
    low, high, mine = ranges(hid, ep, placement_ref, count_ref)
    sel_a[...] = select_a(ep, low, high)
    a_to_peers(0)
    a_sum_cores(3)
    a_pass_on(2)
    r, s = iotas(512, 512)
    block = ((x + ring_offset((r // 64) % 4)) % 4) * 2 + jnp.where(r < 256, 1 - core, core)
    arrange[...] = onehot(
        s == (r % 16) * 32 + ((r // 32) % 2) * 16 + ((r // 16) % 2) * 8 + block
    )
    put_a[...] = place_a(mine)
    put_copy.start()
    sel_b[...] = select_b(low, high)
    a_to_peers(1)
    a_pass_on(3)

    wait_bytes(rcv.at[pl.ds(0, OTHERS)], src_recv)
    lhs_b[...] = dot(arrange[...], rcv[...].reshape(512, PIECE)).astype(BF)
    b_multiply(0)
    a_to_owners(0)
    a_to_peers(2)

    stages = ((b_sum_cores, 0), (b_multiply, -1), (b_pass_on, 1), (b_to_owners, 2))
    extras = {
        0: (lambda: a_to_owners(1), lambda: a_to_peers(3)),
        1: (lambda: a_to_owners(2),),
        2: (lambda: a_to_owners(3),),
        B_CHUNKS - 1: (lambda: c_multiply(0),),
    }

    @pl.loop(0, B_CHUNKS)
    def _(t):
        for stage, lag in stages:
            @pl.when((t >= lag) & (t < B_CHUNKS + lag))
            def _():
                stage(t - lag)
        for at, work in extras.items():
            @pl.when(t == at)
            def _():
                for one in work:
                    one()

    c_sum_cores(0)
    c_multiply(1)
    b_pass_on(B_CHUNKS - 1)
    b_to_owners(B_CHUNKS - 2)
    c_sum_cores(1)
    c_pass_on(0)
    b_to_owners(B_CHUNKS - 1)
    c_pass_on(1)
    c_to_owners(0)
    c_to_owners(1)

    rest = pl.ds(0, OTHERS)
    put_copy.wait()
    wait_bytes(src.at[rest], src_send)
    for c in range(A_CHUNKS):
        a_core(c).wait_send()
        wait_bytes(a_own[c].at[pl.ds(0, 96)], a_x_send.at[c])
        wait_bytes(a_sum[c].at[rest], a_in_send.at[c])
        wait_bytes(a_pick[c].at[rest], a_own_send.at[c])
        a_keep(c).wait()
        wait_bytes(a_got[c].at[rest], a_own_recv.at[c])
    wait_bytes(b_core_out, b_core_send)
    wait_bytes(b_own.at[:, pl.ds(0, 192)], b_x_send)
    wait_bytes(b_pick.at[:, rest], b_own_send)
    wait_bytes(b_pick.at[:, 0], b_self)
    wait_bytes(b_got.at[:, rest], b_own_recv)
    for n in range(C_CHUNKS):
        c_core(n).wait_send()
        wait_bytes(c_own[n].at[pl.ds(0, 192)], c_x_send.at[n])
        wait_bytes(c_pick[n].at[rest], c_own_send.at[n])
        c_keep(n).wait()
        wait_bytes(c_got[n].at[rest], c_own_recv.at[n])


def place_kernel(*refs):
    refs = list(refs)

    def take(count):
        taken = refs[:count]
        del refs[:count]
        return taken

    a_got, (b_got,), c_got, (put_hbm, out_hbm) = take(A_CHUNKS), take(1), take(C_CHUNKS), take(2)
    a_in, (b_in,), c_in, (put_a,) = take(A_CHUNKS), take(1), take(C_CHUNKS), take(1)
    a_out, b_out, put_load, a_load, b_load, c_load, a_sem, b_sem, c_sem = refs

    chunks = [
        (b_got.at[n], b_in.at[n], b_load.at[n], b_sem.at[n], n * B_WIDTH, B_WIDTH)
        for n in range(B_CHUNKS)
    ] + [
        (c_got[n], c_in[n], c_load.at[n], c_sem.at[n], C_START + n * C_WIDTH, C_WIDTH)
        for n in range(C_CHUNKS)
    ]
    put_copy = pltpu.make_async_copy(put_hbm, put_a, put_load)
    a_reads = [pltpu.make_async_copy(a_got[c], a_in[c], a_load.at[c]) for c in range(A_CHUNKS)]
    reads = [pltpu.make_async_copy(got, held, load) for got, held, load, *_ in chunks]
    stores = []
    put_copy.start()
    for copy in a_reads + reads:
        copy.start()
    r, s = iotas(256, 256)
    put_b = onehot(s == (r % 16) * 16 + ((r // 16) % 4) * 4 + r // 64)
    put_copy.wait()
    for c in range(A_CHUNKS):
        a_reads[c].wait()
        columns = pl.ds(A_STARTS[c], A_WIDTHS[c])
        both = jnp.concatenate([
            jnp.concatenate([a_in[c][m * 8 + q] for q in range(8)], axis=1) for m in range(2)
        ], axis=0)
        a_out[:, columns] = dot(put_a[...], both).astype(BF)
        stores.append(
            pltpu.make_async_copy(a_out.at[:, columns], out_hbm.at[0, :, columns], a_sem.at[c])
        )
        stores[-1].start()
    for read, (_, held, _, sem, start, width) in zip(reads, chunks):
        read.wait()
        quarter = width // 4
        rows = dot(put_b, held[...].reshape(256, 2 * quarter)).astype(BF)
        for k in range(2):
            for g in range(4):
                first = start + g * quarter
                b_out[k, :, first:first + quarter] = rows[
                    g * 64:(g + 1) * 64, k * quarter:(k + 1) * quarter
                ]
        columns = pl.ds(start, width)
        stores.append(
            pltpu.make_async_copy(
                b_out.at[:, :, columns], out_hbm.at[pl.ds(1, 2), :, columns], sem
            )
        )
        stores[-1].start()
    for copy in stores:
        copy.wait()


def on_device(gate_proj, up_proj, down_proj, rotation, placement, row_count):
    dma = pltpu.SemaphoreType.DMA
    smem = pl.BlockSpec(memory_space=pltpu.SMEM)
    hbm = pl.BlockSpec(memory_space=pl.ANY)

    def held(*shape):
        return pltpu.VMEM(shape, BF)

    def per_a(shape_of):
        return [held(*shape_of(w)) for w in A_WIDTHS]

    b = B_CHUNKS
    c = C_CHUNKS
    one = dma
    each_a, each_b, each_c = dma((A_CHUNKS,)), dma((b,)), dma((c,))
    scratch = [
        held(*gate_proj.shape), held(*up_proj.shape), held(*down_proj.shape),
        held(PIECE, HIDDEN), held(256, PIECE), held(512, PIECE),
        held(16, 2, 16, PIECE), held(16, 2, 16, PIECE),
        held(512, 256), held(64, 64), held(256, 128), held(512, 512),
        *per_a(lambda w: (128, w)),
        *per_a(lambda w: (128, w)),
        *per_a(lambda w: (128, w)),
        *per_a(lambda w: (2, 16, w)),
        *per_a(lambda w: (2, 32, w)),
        *per_a(lambda w: (16, 16, w // 8)),
        *per_a(lambda w: (16, 16, w // 8)),
        *per_a(lambda w: (16, 32, w // 8)),
        held(b, 256, B_WIDTH), held(b, 256, B_WIDTH), held(b, 256, B_WIDTH),
        held(b, 2, 32, B_WIDTH), held(b, 2, 64, B_WIDTH), held(b, 16, 16, B_WIDTH // 2),
        *[held(256, C_WIDTH)] * (3 * c),
        *[held(2, 32, C_WIDTH)] * c, *[held(2, 64, C_WIDTH)] * c, *[held(16, 16, C_WIDTH // 2)] * c,
        dma((3,)), each_a, one, one, one,
        *[each_a] * 10,
        one, each_b, one, each_b, each_b,
        one, one, one,
        *[each_c] * 8,
    ]
    arrived = [
        *(jax.ShapeDtypeStruct((16, 32, w // 8), BF) for w in A_WIDTHS),
        jax.ShapeDtypeStruct((b, 16, 16, B_WIDTH // 2), BF),
        *[jax.ShapeDtypeStruct((16, 16, C_WIDTH // 2), BF)] * c,
        jax.ShapeDtypeStruct((64, 64), BF),
    ]
    limit = 60 * 1024 * 1024
    got = pl.pallas_call(
        kernel,
        out_shape=arrived,
        in_specs=[smem, smem, hbm, hbm, hbm, hbm],
        out_specs=[hbm] * len(arrived),
        scratch_shapes=scratch,
        compiler_params=pltpu.CompilerParams(
            collective_id=0, has_side_effects=True, vmem_limit_bytes=limit
        ),
        name="rotate_and_send",
    )(placement, row_count, gate_proj, up_proj, down_proj, rotation)
    out = pl.pallas_call(
        place_kernel,
        out_shape=jax.ShapeDtypeStruct((3, 64, HIDDEN), BF),
        in_specs=[hbm] * len(got),
        out_specs=hbm,
        scratch_shapes=[
            *(held(*v.shape) for v in arrived),
            held(64, HIDDEN), held(2, 64, HIDDEN),
            one, each_a, each_b, each_c, each_a, each_b, each_c,
        ],
        compiler_params=pltpu.CompilerParams(vmem_limit_bytes=limit),
        name="place",
    )(*got)
    return jnp.transpose(out, (1, 0, 2))[None]


def solution(mesh):
    in_specs = (
        P(None, "hid", "ep"),
        P(None, "hid", "ep"),
        P(None, "ep", "hid"),
        P("hid", None),
        P(),
        P(),
    )
    out_specs = P("ep", "hid", None, None)
    return jax.shard_map(
        on_device, mesh=mesh, in_specs=in_specs, out_specs=out_specs, check_vma=False
    )
```

```python
import jax
import jax.numpy as jnp
from jax import lax
from jax.experimental import pallas as pl
from jax.experimental.pallas import tpu as pltpu
from jax.sharding import PartitionSpec as P

MESH = pl.DeviceIdType.MESH
BF = jnp.bfloat16
F32 = jnp.float32
PEERS = (
    (0, 1), (0, 3), (1, 0), (3, 0), (1, 1), (3, 3), (1, 3), (3, 1),
    (0, 2), (2, 0), (1, 2), (2, 1), (3, 2), (2, 3), (2, 2),
)
OTHERS = len(PEERS)
HIDDEN = 7168
PIECE = 896
A_WIDTHS = (1024, 2048, 2048, 2048)
A_STARTS = (0, 1024, 3072, 5120)
A_CHUNKS = len(A_WIDTHS)
B_WIDTH = 1024
B_CHUNKS = 6
C_WIDTH = 512
C_START = B_CHUNKS * B_WIDTH
C_CHUNKS = (HIDDEN - C_START) // C_WIDTH
TILE = 1024


def iotas(rows, cols):
    return (
        lax.broadcasted_iota(jnp.int32, (rows, cols), 0),
        lax.broadcasted_iota(jnp.int32, (rows, cols), 1),
    )


def onehot(condition):
    return jnp.where(condition, 1.0, 0.0).astype(BF)


def dot(a, b):
    return jnp.dot(a, b, preferred_element_type=F32)


def dot_t(a, b):
    return lax.dot_general(a, b, (((1,), (1,)), ((), ())), preferred_element_type=F32)


def ring_offset(index):
    return jnp.where(index == 0, 2, jnp.where(index == 1, 1, jnp.where(index == 2, 3, 0)))


def ranges(h, ep, placement_ref, count_ref):
    owners, _ = iotas(16, 256)
    low, high, mine = [], [], []
    for m in range(2):
        start = jnp.int32(0)
        count = jnp.int32(0)
        lo = jnp.zeros((16, 256), jnp.int32)
        hi = jnp.zeros((16, 256), jnp.int32)
        for t in range(16):
            o = placement_ref[m, t]
            end = start + lax.shift_right_logical(count_ref[m, o], 4)
            first = lax.shift_right_logical(start + 7 - h, 3)
            last = lax.shift_right_logical(end + 7 - h, 3)
            lo = jnp.where(owners == o, first, lo)
            hi = jnp.where(owners == o, last, hi)
            count = jnp.where(o == ep, last - first, count)
            start = end
        low.append(lo)
        high.append(hi)
        mine.append(count)
    return low, high, mine


def select_a(ep, low, high):
    first = ep < 8
    lo = jnp.where(first, low[0], low[1])
    hi = jnp.where(first, high[0], high[1])
    _, col = iotas(16, 256)
    e = col // 16
    place = jnp.where((lo <= e) & (e < hi), e - lo, -1)
    place = jnp.broadcast_to(place[:, None, :], (16, 32, 256)).reshape(512, 256)
    r, s = iotas(512, 256)
    return onehot((place == (r // 16) % 2) & (r % 16 == s % 16))


def place_a(mine):
    r, s = iotas(64, 64)
    slot = (s // 16) % 2 + jnp.where(s < 32, 0, mine[0])
    return onehot((slot == r // 16) & (r % 16 == s % 16))


def select_b(low, high):
    _, col = iotas(16, 128)
    m = (col // 16) % 2
    e = col % 16
    low = [v[:, :128] for v in low]
    high = [v[:, :128] for v in high]
    lo = jnp.where(m == 0, low[0], low[1])
    hi = jnp.where(m == 0, high[0], high[1])
    slot = e - lo + jnp.where(m == 0, 0, high[0] - low[0])
    slot = jnp.where((lo <= e) & (e < hi), slot, -1)
    slot = jnp.broadcast_to(slot[:, None, :], (16, 16, 128)).reshape(256, 128)
    r, s = iotas(256, 128)
    return onehot((slot == (r // 4) % 4) & (r % 4 == s // 32))


def order_owner_rows():
    r, s = iotas(256, 256)
    return onehot(s == (r % 16) * 16 + ((r // 16) % 4) * 4 + r // 64)


def place_rows(put_b, got, out):
    width = got.shape[-1] // 2
    rows = dot(put_b, got[...].reshape(256, 2 * width)).astype(BF)
    for k in range(2):
        for g in range(4):
            out[k, :, g * width:(g + 1) * width] = rows[
                g * 64:(g + 1) * 64, k * width:(k + 1) * width
            ]


def kernel(
    placement_ref, count_ref, gate_hbm, up_hbm, down_hbm, rot_hbm, *scratch
):
    scratch = list(scratch)

    def take(count):
        taken = scratch[:count]
        del scratch[:count]
        return taken

    part_hbm, last_got = take(2)
    gate, up, down = take(3)
    rot, lhs_a, lhs_b, src, rcv, sel_a, put_a, sel_b, put_b, arrange = take(10)
    a_core_out, a_core_in, a_own, a_far, a_near, a_sum, a_in, a_pick, a_got = (
        take(A_CHUNKS) for _ in range(9)
    )
    b_core_out, b_core_in, b_own, b_far, b_near, b_pick, b_got = take(7)
    c_core_out, c_core_in, c_own, c_far, c_near, c_pick = (take(C_CHUNKS) for _ in range(6))
    c_got = take(C_CHUNKS - 1) + [last_got]
    a_out, b_out, c_out = take(3)
    in_sem, rot_sem, src_send, src_recv = take(4)
    a_store_sem, b_store_sem, c_store_sem = take(3)
    a_core_send, a_core_recv, a_x_send, a_far_recv, a_near_recv = take(5)
    a_in_send, a_in_recv, a_own_send, a_own_recv = take(4)
    b_core_send, b_core_recv, b_x_send, b_far_recv, b_near_recv = take(5)
    b_own_send, b_own_recv = take(2)
    c_core_send, c_core_recv, c_x_send, c_far_recv, c_near_recv = take(5)
    c_own_send, c_own_recv, c_self = take(3)

    hid = lax.axis_index("hid")
    ep = lax.axis_index("ep")
    x, core = hid // 2, hid % 2
    z, y = ep // 4, ep % 4
    right = lax.rem(x + 1, 4) * 2 + core
    left = lax.rem(x + 3, 4) * 2 + core
    other = x * 2 + 1 - core
    peers = [lax.rem(z + dz, 4) * 4 + lax.rem(y + dy, 4) for dz, dy in PEERS]

    def remote(source, target, send, recv, h, e):
        return pltpu.make_async_remote_copy(
            source, target, send, recv, device_id=(h, e), device_id_type=MESH
        )

    def wait_bytes(ref, sem):
        pltpu.make_async_copy(ref, ref, sem).wait()

    barrier = pltpu.get_barrier_semaphore()
    for h in (right, left, other):
        pl.semaphore_signal(barrier, 1, device_id=(h, ep), device_id_type=MESH)
    for p in peers:
        pl.semaphore_signal(barrier, 1, device_id=(hid, p), device_id_type=MESH)

    def rot_copy(c):
        columns = pl.ds(A_STARTS[c], A_WIDTHS[c])
        return pltpu.make_async_copy(rot_hbm.at[:, columns], rot.at[:, columns], rot_sem.at[c])

    def src_copy(i):
        return remote(
            src.at[peers[i]], rcv.at[ep], src_send, src_recv, hid, peers[i]
        )

    def x_copy(own, far, near, send, far_recv, near_recv, half, i):
        first, to, target, recv = (
            (0, right, far.at[0], far_recv),
            (1, left, far.at[1], far_recv),
            (3, right, near.at[0, pl.ds(half, half)], near_recv),
            (4, left, near.at[1, pl.ds(0, half)], near_recv),
            (2, right, near.at[0, pl.ds(0, half)], near_recv),
            (5, left, near.at[1, pl.ds(half, half)], near_recv),
        )[i]
        return remote(own.at[pl.ds(first * half, half)], target, send, recv, to, ep)

    def a_x(c, i):
        return x_copy(
            a_own[c], a_far[c], a_near[c],
            a_x_send.at[c], a_far_recv.at[c], a_near_recv.at[c], 16, i,
        )

    def b_x(n, i):
        return x_copy(
            b_own.at[n], b_far.at[n], b_near.at[n],
            b_x_send, b_far_recv.at[n], b_near_recv.at[n], 32, i,
        )

    def c_x(n, i):
        return x_copy(
            c_own[n], c_far[n], c_near[n],
            c_x_send.at[n], c_far_recv.at[n], c_near_recv.at[n], 32, i,
        )

    def c_core(n):
        return remote(c_core_out[n], c_core_in[n], c_core_send.at[n], c_core_recv.at[n], other, ep)

    def c_owner(n, i):
        return remote(
            c_pick[n].at[peers[i]], c_got[n].at[ep], c_own_send.at[n], c_own_recv.at[n],
            hid, peers[i],
        )

    def last_keep():
        return pltpu.make_async_copy(c_pick[-1].at[ep], last_got.at[ep], c_self)

    def a_core(c):
        return remote(a_core_out[c], a_core_in[c], a_core_send.at[c], a_core_recv.at[c], other, ep)

    def b_core(n):
        return remote(
            b_core_out.at[n], b_core_in.at[n], b_core_send, b_core_recv.at[n], other, ep
        )

    def a_spread(c, i):
        return remote(
            a_sum[c].at[peers[i]], a_in[c].at[ep], a_in_send.at[c], a_in_recv.at[c], hid, peers[i]
        )

    def a_owner(c, i):
        return remote(
            a_pick[c].at[peers[i]], a_got[c].at[ep], a_own_send.at[c], a_own_recv.at[c],
            hid, peers[i],
        )

    def b_owner(n, i):
        return remote(
            b_pick.at[n, peers[i]], b_got.at[n, ep], b_own_send, b_own_recv.at[n], hid, peers[i]
        )

    def a_store(c):
        columns = pl.ds(A_STARTS[c], A_WIDTHS[c])
        return pltpu.make_async_copy(
            a_out.at[:, columns], part_hbm.at[0, :, columns], a_store_sem.at[c]
        )

    def b_store(n):
        columns = pl.ds(pl.multiple_of(n * B_WIDTH, B_WIDTH), B_WIDTH)
        return pltpu.make_async_copy(
            b_out.at[n], part_hbm.at[pl.ds(1, 2), :, columns], b_store_sem
        )

    def c_store(n):
        columns = pl.ds(C_START + n * C_WIDTH, C_WIDTH)
        return pltpu.make_async_copy(
            c_out.at[n], part_hbm.at[pl.ds(1, 2), :, columns], c_store_sem.at[n]
        )

    in_copies = [
        pltpu.make_async_copy(source, target, in_sem.at[i])
        for i, (source, target) in enumerate(((gate_hbm, gate), (up_hbm, up), (down_hbm, down)))
    ]

    def sum_cores(own, core_in, half, start_x):
        own[0:2 * half] += core_in[0:2 * half]
        start_x(0)
        start_x(1)
        own[2 * half:6 * half] += core_in[2 * half:6 * half]
        start_x(2)
        start_x(3)
        own[6 * half:8 * half] += core_in[6 * half:8 * half]

    def pass_on(own, far, far_recv, half, x_of):
        wait_bytes(far, far_recv)
        own[2 * half:3 * half] += far[0]
        x_of(4).start()
        own[5 * half:6 * half] += far[1]
        x_of(5).start()

    def total_of(own, near, half, rows, columns):
        return (
            own[6 * half + rows.start:6 * half + rows.stop, columns].astype(F32)
            + near[0, rows, columns].astype(F32)
            + near[1, rows, columns].astype(F32)
        ).astype(BF)

    def a_multiply(c):
        rot_copy(c).wait()
        if c + 1 < A_CHUNKS:
            rot_copy(c + 1).start()

        @pl.loop(0, A_WIDTHS[c] // TILE)
        def _(t):
            here = pl.ds(pl.multiple_of(t * TILE, TILE), TILE)
            there = pl.ds(pl.multiple_of(A_STARTS[c] + t * TILE, TILE), TILE)
            total = dot(lhs_a[...], rot[:, there])
            a_core_out[c][:, here] = total[:128].astype(BF)
            a_own[c][:, here] = total[128:].astype(BF)

    def a_sum_cores(c):
        a_core(c).wait_recv()
        sum_cores(a_own[c], a_core_in[c], 16, lambda i: a_x(c, i).start())

    def a_pass_on(c):
        pass_on(a_own[c], a_far[c], a_far_recv.at[c], 16, lambda i: a_x(c, i))

    def a_to_peers(c):
        wait_bytes(a_near[c], a_near_recv.at[c])
        eighth = A_WIDTHS[c] // 8
        for m in range(2):
            for q in range(8):
                a_sum[c][m * 8 + q] = total_of(
                    a_own[c], a_near[c], 16,
                    slice(m * 16, m * 16 + 16), slice(q * eighth, (q + 1) * eighth),
                )
        for i in range(OTHERS):
            a_spread(c, i).start()
        a_in[c][ep] = a_sum[c][ep]

    def a_to_owners(c):
        wait_bytes(a_in[c].at[pl.ds(0, OTHERS)], a_in_recv.at[c])
        eighth = A_WIDTHS[c] // 8
        rows = dot(sel_a[...], a_in[c][...].reshape(256, eighth))
        a_pick[c][...] = rows.astype(BF).reshape(16, 32, eighth)
        for i in range(OTHERS):
            a_owner(c, i).start()
        a_got[c][ep] = a_pick[c][ep]

    def a_place(c):
        wait_bytes(a_got[c].at[pl.ds(0, OTHERS)], a_own_recv.at[c])
        both = jnp.concatenate([
            jnp.concatenate([a_got[c][m * 8 + q] for q in range(8)], axis=1) for m in range(2)
        ], axis=0)
        a_out[:, pl.ds(A_STARTS[c], A_WIDTHS[c])] = dot(put_a[...], both).astype(BF)
        a_store(c).start()

    def multiply(width, start, core_out, own):
        total = dot(lhs_b[...], rot[:, pl.ds(start, width)])
        core_out[...] = total[:256].astype(BF)
        own[...] = total[256:].astype(BF)

    def pick_rows(width, own, near, pick):
        quarter = width // 4
        quarters = []
        for g in range(4):
            columns = slice(g * quarter, (g + 1) * quarter)
            quarters.append(jnp.concatenate([
                total_of(own, near, 32, slice(k * 32, k * 32 + 32), columns) for k in range(2)
            ], axis=1))
        rows = dot(sel_b[...], jnp.concatenate(quarters, axis=0))
        pick[...] = rows.astype(BF).reshape(16, 16, 2 * quarter)

    def b_multiply(n):
        start = pl.multiple_of(n * B_WIDTH, B_WIDTH)
        multiply(B_WIDTH, start, b_core_out.at[n], b_own.at[n])
        b_core(n).start()

    def b_sum_cores(n):
        b_core(n).wait_recv()
        sum_cores(b_own.at[n], b_core_in.at[n], 32, lambda i: b_x(n, i).start())

    def b_pass_on(n):
        pass_on(b_own.at[n], b_far.at[n], b_far_recv.at[n], 32, lambda i: b_x(n, i))

    def b_to_owners(n):
        wait_bytes(b_near.at[n], b_near_recv.at[n])
        pick_rows(B_WIDTH, b_own.at[n], b_near.at[n], b_pick.at[n])
        for i in range(OTHERS):
            b_owner(n, i).start()
        b_got[n, ep] = b_pick[n, ep]

    def b_place(n):
        wait_bytes(b_got.at[n, pl.ds(0, OTHERS)], b_own_recv.at[n])
        place_rows(put_b[...], b_got.at[n], b_out.at[n])
        b_store(n).start()

    def c_multiply(n):
        multiply(C_WIDTH, C_START + n * C_WIDTH, c_core_out[n], c_own[n])
        c_core(n).start()

    def c_sum_cores(n):
        c_core(n).wait_recv()
        sum_cores(c_own[n], c_core_in[n], 32, lambda i: c_x(n, i).start())

    def c_pass_on(n):
        pass_on(c_own[n], c_far[n], c_far_recv.at[n], 32, lambda i: c_x(n, i))

    def c_to_owners(n):
        wait_bytes(c_near[n], c_near_recv.at[n])
        pick_rows(C_WIDTH, c_own[n], c_near[n], c_pick[n])
        for i in range(OTHERS):
            c_owner(n, i).start()
        if n < C_CHUNKS - 1:
            c_got[n][ep] = c_pick[n][ep]
        else:
            last_keep().start()

    def c_place(n):
        wait_bytes(c_got[n].at[pl.ds(0, OTHERS)], c_own_recv.at[n])
        place_rows(put_b[...], c_got[n], c_out.at[n])
        c_store(n).start()

    in_copies[0].start()
    rot_copy(0).start()
    in_copies[1].start()
    in_copies[2].start()

    r, s = iotas(256, 128)
    block = ((x + ring_offset((r // 32) % 4)) % 4) * 2 + jnp.where(r < 128, 1 - core, core)
    column = block * 16 + r % 16
    expert = (r // 16) % 2
    in_copies[0].wait()
    rows = sum(dot_t(onehot((expert == m) & (s == column)), gate[m]) for m in range(2))
    lhs_a[...] = rows.astype(BF)

    a_multiply(0)

    pl.semaphore_wait(barrier, 3 + OTHERS)

    a_core(0).start()
    column = (r % 8) * 16 + r // 16
    expert = (r // 8) % 2
    spread = [onehot((expert == m) & (s == column)) for m in range(2)]
    in_copies[1].wait()
    rows = sum(dot_t(spread[m], up[m]) for m in range(2))
    src[:, 0] = rows.astype(BF).reshape(16, 16, PIECE)
    in_copies[2].wait()
    rows = sum(dot(spread[m], down[m]) for m in range(2))
    src[:, 1] = rows.astype(BF).reshape(16, 16, PIECE)
    for i in range(OTHERS):
        src_copy(i).start()
    a_sum_cores(0)
    a_multiply(1)
    a_core(1).start()
    a_multiply(2)
    a_core(2).start()
    a_sum_cores(1)
    a_pass_on(0)
    a_multiply(3)
    a_core(3).start()
    a_sum_cores(2)
    a_pass_on(1)
    rcv[ep] = src[ep]
    low, high, mine = ranges(hid, ep, placement_ref, count_ref)
    sel_a[...] = select_a(ep, low, high)
    a_to_peers(0)
    a_sum_cores(3)
    a_pass_on(2)
    r, s = iotas(512, 512)
    block = ((x + ring_offset((r // 64) % 4)) % 4) * 2 + jnp.where(r < 256, 1 - core, core)
    arrange[...] = onehot(
        s == (r % 16) * 32 + ((r // 32) % 2) * 16 + ((r // 16) % 2) * 8 + block
    )
    put_a[...] = place_a(mine)
    put_b[...] = order_owner_rows()
    sel_b[...] = select_b(low, high)
    a_to_peers(1)
    a_pass_on(3)

    wait_bytes(rcv.at[pl.ds(0, OTHERS)], src_recv)
    lhs_b[...] = dot(arrange[...], rcv[...].reshape(512, PIECE)).astype(BF)
    b_multiply(0)
    a_to_owners(0)
    a_to_peers(2)

    stages = (
        (b_sum_cores, 0), (b_multiply, -1), (b_pass_on, 1), (b_to_owners, 2), (b_place, 5),
    )
    extras = {
        0: (lambda: a_to_owners(1), lambda: a_to_peers(3)),
        1: (lambda: a_to_owners(2),),
        2: (lambda: a_to_owners(3),),
        3: (lambda: a_place(0),),
        4: (lambda: a_place(1),),
        B_CHUNKS - 1: (lambda: c_multiply(0), lambda: c_multiply(1)),
    }

    @pl.loop(0, B_CHUNKS)
    def _(t):
        for stage, lag in stages:
            @pl.when((t >= lag) & (t < B_CHUNKS + lag))
            def _():
                stage(t - lag)
        for at, work in extras.items():
            @pl.when(t == at)
            def _():
                for one in work:
                    one()

    c_sum_cores(0)
    b_pass_on(B_CHUNKS - 1)
    c_sum_cores(1)
    b_to_owners(B_CHUNKS - 2)
    c_pass_on(0)
    b_to_owners(B_CHUNKS - 1)
    c_pass_on(1)
    a_place(2)
    c_to_owners(0)
    a_place(3)
    b_place(1)
    c_to_owners(1)
    for n in range(2, B_CHUNKS):
        b_place(n)
    c_place(0)

    rest = pl.ds(0, OTHERS)
    wait_bytes(src.at[rest], src_send)
    for c in range(A_CHUNKS):
        a_core(c).wait_send()
        wait_bytes(a_own[c].at[pl.ds(0, 96)], a_x_send.at[c])
        wait_bytes(a_sum[c].at[rest], a_in_send.at[c])
        wait_bytes(a_pick[c].at[rest], a_own_send.at[c])
        a_store(c).wait()
    wait_bytes(b_core_out, b_core_send)
    wait_bytes(b_own.at[:, pl.ds(0, 192)], b_x_send)
    wait_bytes(b_pick.at[:, rest], b_own_send)
    for n in range(C_CHUNKS):
        c_core(n).wait_send()
        wait_bytes(c_own[n].at[pl.ds(0, 192)], c_x_send.at[n])
        wait_bytes(c_pick[n].at[rest], c_own_send.at[n])
    last_keep().wait()
    wait_bytes(b_out, b_store_sem)
    c_store(0).wait()
    wait_bytes(last_got.at[rest], c_own_recv.at[C_CHUNKS - 1])


def place_kernel(part_hbm, last_got, out_hbm, got, held, load, got_load, store):
    last = HIDDEN - C_WIDTH
    pieces = [(pl.ds(0, 3), n * 1024, 1024) for n in range(last // 1024)]
    pieces.append((pl.ds(0, 3), last - last % 1024, last % 1024))
    pieces.append((pl.ds(0, 1), last, C_WIDTH))
    pieces = [(kinds, slice(None), pl.ds(start, width)) for kinds, start, width in pieces]
    loads = [
        pltpu.make_async_copy(part_hbm.at[at], held.at[at], load.at[i])
        for i, at in enumerate(pieces)
    ]
    pieces.append((pl.ds(1, 2), slice(None), pl.ds(last, C_WIDTH)))
    stores = [
        pltpu.make_async_copy(held.at[at], out_hbm.at[at], store.at[i])
        for i, at in enumerate(pieces)
    ]
    got_copy = pltpu.make_async_copy(last_got, got, got_load)
    got_copy.start()
    for copy in loads:
        copy.start()
    put_b = order_owner_rows()
    for load, store in zip(loads[:4], stores[:4]):
        load.wait()
        store.start()
    got_copy.wait()
    place_rows(put_b, got, held.at[pl.ds(1, 2), :, pl.ds(last, C_WIDTH)])
    stores[-1].start()
    for load, store in zip(loads[4:], stores[4:]):
        load.wait()
        store.start()
    for copy in stores:
        copy.wait()


def on_device(gate_proj, up_proj, down_proj, rotation, placement, row_count):
    dma = pltpu.SemaphoreType.DMA
    smem = pl.BlockSpec(memory_space=pltpu.SMEM)
    hbm = pl.BlockSpec(memory_space=pl.ANY)

    def held(*shape):
        return pltpu.VMEM(shape, BF)

    def per_a(shape_of):
        return [held(*shape_of(w)) for w in A_WIDTHS]

    b = B_CHUNKS
    c = C_CHUNKS
    one = dma
    each_a, each_b, each_c = dma((A_CHUNKS,)), dma((b,)), dma((c,))
    scratch = [
        held(*gate_proj.shape), held(*up_proj.shape), held(*down_proj.shape),
        held(PIECE, HIDDEN), held(256, PIECE), held(512, PIECE),
        held(16, 2, 16, PIECE), held(16, 2, 16, PIECE),
        held(512, 256), held(64, 64), held(256, 128), held(256, 256), held(512, 512),
        *per_a(lambda w: (128, w)),
        *per_a(lambda w: (128, w)),
        *per_a(lambda w: (128, w)),
        *per_a(lambda w: (2, 16, w)),
        *per_a(lambda w: (2, 32, w)),
        *per_a(lambda w: (16, 16, w // 8)),
        *per_a(lambda w: (16, 16, w // 8)),
        *per_a(lambda w: (16, 32, w // 8)),
        *per_a(lambda w: (16, 32, w // 8)),
        held(b, 256, B_WIDTH), held(b, 256, B_WIDTH), held(b, 256, B_WIDTH),
        held(b, 2, 32, B_WIDTH), held(b, 2, 64, B_WIDTH),
        held(b, 16, 16, B_WIDTH // 2), held(b, 16, 16, B_WIDTH // 2),
        *[held(256, C_WIDTH)] * (3 * c),
        *[held(2, 32, C_WIDTH)] * c, *[held(2, 64, C_WIDTH)] * c, *[held(16, 16, C_WIDTH // 2)] * c,
        *[held(16, 16, C_WIDTH // 2)] * (c - 1),
        held(64, HIDDEN), held(b, 2, 64, B_WIDTH), held(c, 2, 64, C_WIDTH),
        dma((3,)), each_a, one, one,
        each_a, one, each_c,
        *[each_a] * 9,
        one, each_b, one, each_b, each_b,
        one, each_b,
        *[each_c] * 7, one,
    ]
    arrived = [
        jax.ShapeDtypeStruct((3, 64, HIDDEN), BF),
        jax.ShapeDtypeStruct((16, 16, C_WIDTH // 2), BF),
    ]
    part, last_got = pl.pallas_call(
        kernel,
        out_shape=arrived,
        in_specs=[smem, smem, hbm, hbm, hbm, hbm],
        out_specs=[hbm] * len(arrived),
        scratch_shapes=scratch,
        compiler_params=pltpu.CompilerParams(
            collective_id=0, has_side_effects=True, vmem_limit_bytes=56 * 1024 * 1024
        ),
        name="rotate_and_send",
    )(placement, row_count, gate_proj, up_proj, down_proj, rotation)
    out = pl.pallas_call(
        place_kernel,
        out_shape=jax.ShapeDtypeStruct((3, 64, HIDDEN), BF),
        in_specs=[hbm] * 2,
        out_specs=hbm,
        scratch_shapes=[
            held(16, 16, C_WIDTH // 2), held(3, 64, HIDDEN), dma((9,)), one, dma((10,)),
        ],
        compiler_params=pltpu.CompilerParams(vmem_limit_bytes=60 * 1024 * 1024),
        name="place",
    )(part, last_got)
    return jnp.transpose(out, (1, 0, 2))[None]


def solution(mesh):
    in_specs = (
        P(None, "hid", "ep"),
        P(None, "hid", "ep"),
        P(None, "ep", "hid"),
        P("hid", None),
        P(),
        P(),
    )
    out_specs = P("ep", "hid", None, None)
    return jax.shard_map(
        on_device, mesh=mesh, in_specs=in_specs, out_specs=out_specs, check_vma=False
    )
```

```python
import jax
import jax.numpy as jnp
from jax import lax
from jax.experimental import pallas as pl
from jax.experimental.pallas import tpu as pltpu
from jax.sharding import PartitionSpec as P

MESH = pl.DeviceIdType.MESH
BF = jnp.bfloat16
F32 = jnp.float32
PEERS = (
    (0, 1), (0, 3), (1, 0), (3, 0), (1, 1), (3, 3), (1, 3), (3, 1),
    (0, 2), (2, 0), (1, 2), (2, 1), (3, 2), (2, 3), (2, 2),
)
OTHERS = len(PEERS)
HIDDEN = 7168
PIECE = 896
A_WIDTHS = (1024, 2048, 2048, 2048)
A_STARTS = (0, 1024, 3072, 5120)
A_CHUNKS = len(A_WIDTHS)
B_WIDTH = 1024
B_CHUNKS = 6
C_WIDTH = 512
C_START = B_CHUNKS * B_WIDTH
C_CHUNKS = (HIDDEN - C_START) // C_WIDTH
TILE = 1024


def iotas(rows, cols):
    return (
        lax.broadcasted_iota(jnp.int32, (rows, cols), 0),
        lax.broadcasted_iota(jnp.int32, (rows, cols), 1),
    )


def onehot(condition):
    return jnp.where(condition, 1.0, 0.0).astype(BF)


def dot(a, b):
    return jnp.dot(a, b, preferred_element_type=F32)


def dot_t(a, b):
    return lax.dot_general(a, b, (((1,), (1,)), ((), ())), preferred_element_type=F32)


def ring_offset(index):
    return jnp.where(index == 0, 2, jnp.where(index == 1, 1, jnp.where(index == 2, 3, 0)))


def ranges(h, ep, placement_ref, count_ref):
    owners, _ = iotas(16, 256)
    low, high, mine = [], [], []
    for m in range(2):
        start = jnp.int32(0)
        count = jnp.int32(0)
        lo = jnp.zeros((16, 256), jnp.int32)
        hi = jnp.zeros((16, 256), jnp.int32)
        for t in range(16):
            o = placement_ref[m, t]
            end = start + lax.shift_right_logical(count_ref[m, o], 4)
            first = lax.shift_right_logical(start + 7 - h, 3)
            last = lax.shift_right_logical(end + 7 - h, 3)
            lo = jnp.where(owners == o, first, lo)
            hi = jnp.where(owners == o, last, hi)
            count = jnp.where(o == ep, last - first, count)
            start = end
        low.append(lo)
        high.append(hi)
        mine.append(count)
    return low, high, mine


def select_a(ep, low, high):
    first = ep < 8
    lo = jnp.where(first, low[0], low[1])
    hi = jnp.where(first, high[0], high[1])
    _, col = iotas(16, 256)
    e = col // 16
    place = jnp.where((lo <= e) & (e < hi), e - lo, -1)
    place = jnp.broadcast_to(place[:, None, :], (16, 32, 256)).reshape(512, 256)
    r, s = iotas(512, 256)
    return onehot((place == (r // 16) % 2) & (r % 16 == s % 16))


def place_a(mine):
    r, s = iotas(64, 64)
    slot = (s // 16) % 2 + jnp.where(s < 32, 0, mine[0])
    return onehot((slot == r // 16) & (r % 16 == s % 16))


def select_b(low, high):
    _, col = iotas(16, 128)
    m = (col // 16) % 2
    e = col % 16
    low = [v[:, :128] for v in low]
    high = [v[:, :128] for v in high]
    lo = jnp.where(m == 0, low[0], low[1])
    hi = jnp.where(m == 0, high[0], high[1])
    slot = e - lo + jnp.where(m == 0, 0, high[0] - low[0])
    slot = jnp.where((lo <= e) & (e < hi), slot, -1)
    slot = jnp.broadcast_to(slot[:, None, :], (16, 16, 128)).reshape(256, 128)
    r, s = iotas(256, 128)
    return onehot((slot == (r // 4) % 4) & (r % 4 == s // 32))


def order_owner_rows():
    r, s = iotas(256, 256)
    return onehot(s == (r % 16) * 16 + ((r // 16) % 4) * 4 + r // 64)


def place_rows(put_b, got, out):
    width = got.shape[-1] // 2
    rows = dot(put_b, got[...].reshape(256, 2 * width)).astype(BF)
    for k in range(2):
        for g in range(4):
            out[k, :, g * width:(g + 1) * width] = rows[
                g * 64:(g + 1) * 64, k * width:(k + 1) * width
            ]


def kernel(
    placement_ref, count_ref, gate_hbm, up_hbm, down_hbm, rot_hbm, *scratch
):
    scratch = list(scratch)

    def take(count):
        taken = scratch[:count]
        del scratch[:count]
        return taken

    part_hbm, last_got = take(2)
    gate, up, down = take(3)
    rot, lhs_a, lhs_b, src, rcv, sel_a, put_a, sel_b, put_b, arrange = take(10)
    a_core_out, a_core_in, a_own, a_far, a_near, a_sum, a_in, a_pick, a_got = (
        take(A_CHUNKS) for _ in range(9)
    )
    b_core_out, b_core_in, b_own, b_far, b_near, b_pick, b_got = take(7)
    c_core_out, c_core_in, c_own, c_far, c_near, c_pick = (take(C_CHUNKS) for _ in range(6))
    c_got = take(C_CHUNKS - 1) + [last_got]
    a_out, b_out, c_out = take(3)
    in_sem, rot_sem, src_send, src_recv = take(4)
    a_store_sem, b_store_sem, c_store_sem = take(3)
    a_core_send, a_core_recv, a_x_send, a_far_recv, a_near_recv = take(5)
    a_in_send, a_in_recv, a_own_send, a_own_recv = take(4)
    b_core_send, b_core_recv, b_x_send, b_far_recv, b_near_recv = take(5)
    b_own_send, b_own_recv = take(2)
    c_core_send, c_core_recv, c_x_send, c_far_recv, c_near_recv = take(5)
    c_own_send, c_own_recv, c_self = take(3)

    hid = lax.axis_index("hid")
    ep = lax.axis_index("ep")
    x, core = hid // 2, hid % 2
    z, y = ep // 4, ep % 4
    right = lax.rem(x + 1, 4) * 2 + core
    left = lax.rem(x + 3, 4) * 2 + core
    other = x * 2 + 1 - core
    peers = [lax.rem(z + dz, 4) * 4 + lax.rem(y + dy, 4) for dz, dy in PEERS]

    def remote(source, target, send, recv, h, e):
        return pltpu.make_async_remote_copy(
            source, target, send, recv, device_id=(h, e), device_id_type=MESH
        )

    def wait_bytes(ref, sem):
        pltpu.make_async_copy(ref, ref, sem).wait()

    barrier = pltpu.get_barrier_semaphore()
    for h in (right, left, other):
        pl.semaphore_signal(barrier, 1, device_id=(h, ep), device_id_type=MESH)
    for p in peers:
        pl.semaphore_signal(barrier, 1, device_id=(hid, p), device_id_type=MESH)

    def rot_copy(c):
        columns = pl.ds(A_STARTS[c], A_WIDTHS[c])
        return pltpu.make_async_copy(rot_hbm.at[:, columns], rot.at[:, columns], rot_sem.at[c])

    def src_copy(i):
        return remote(
            src.at[peers[i]], rcv.at[ep], src_send, src_recv, hid, peers[i]
        )

    def x_copy(own, far, near, send, far_recv, near_recv, half, i):
        first, to, target, recv = (
            (0, right, far.at[0], far_recv),
            (1, left, far.at[1], far_recv),
            (3, right, near.at[0, pl.ds(half, half)], near_recv),
            (4, left, near.at[1, pl.ds(0, half)], near_recv),
            (2, right, near.at[0, pl.ds(0, half)], near_recv),
            (5, left, near.at[1, pl.ds(half, half)], near_recv),
        )[i]
        return remote(own.at[pl.ds(first * half, half)], target, send, recv, to, ep)

    def a_x(c, i):
        return x_copy(
            a_own[c], a_far[c], a_near[c],
            a_x_send.at[c], a_far_recv.at[c], a_near_recv.at[c], 16, i,
        )

    def b_x(n, i):
        return x_copy(
            b_own.at[n], b_far.at[n], b_near.at[n],
            b_x_send, b_far_recv.at[n], b_near_recv.at[n], 32, i,
        )

    def c_x(n, i):
        return x_copy(
            c_own[n], c_far[n], c_near[n],
            c_x_send.at[n], c_far_recv.at[n], c_near_recv.at[n], 32, i,
        )

    def c_core(n):
        return remote(c_core_out[n], c_core_in[n], c_core_send.at[n], c_core_recv.at[n], other, ep)

    def c_owner(n, i):
        return remote(
            c_pick[n].at[peers[i]], c_got[n].at[ep], c_own_send.at[n], c_own_recv.at[n],
            hid, peers[i],
        )

    def last_keep():
        return pltpu.make_async_copy(c_pick[-1].at[ep], last_got.at[ep], c_self)

    def a_core(c):
        return remote(a_core_out[c], a_core_in[c], a_core_send.at[c], a_core_recv.at[c], other, ep)

    def b_core(n):
        return remote(
            b_core_out.at[n], b_core_in.at[n], b_core_send, b_core_recv.at[n], other, ep
        )

    def a_spread(c, i):
        return remote(
            a_sum[c].at[peers[i]], a_in[c].at[ep], a_in_send.at[c], a_in_recv.at[c], hid, peers[i]
        )

    def a_owner(c, i):
        return remote(
            a_pick[c].at[peers[i]], a_got[c].at[ep], a_own_send.at[c], a_own_recv.at[c],
            hid, peers[i],
        )

    def b_owner(n, i):
        return remote(
            b_pick.at[n, peers[i]], b_got.at[n, ep], b_own_send, b_own_recv.at[n], hid, peers[i]
        )

    def a_store(c):
        columns = pl.ds(A_STARTS[c], A_WIDTHS[c])
        return pltpu.make_async_copy(
            a_out.at[:, columns], part_hbm.at[0, :, columns], a_store_sem.at[c]
        )

    def b_store(n):
        columns = pl.ds(pl.multiple_of(n * B_WIDTH, B_WIDTH), B_WIDTH)
        return pltpu.make_async_copy(
            b_out.at[n], part_hbm.at[pl.ds(1, 2), :, columns], b_store_sem
        )

    def c_store(n):
        columns = pl.ds(C_START + n * C_WIDTH, C_WIDTH)
        return pltpu.make_async_copy(
            c_out.at[n], part_hbm.at[pl.ds(1, 2), :, columns], c_store_sem.at[n]
        )

    in_copies = [
        pltpu.make_async_copy(source, target, in_sem.at[i])
        for i, (source, target) in enumerate(((gate_hbm, gate), (up_hbm, up), (down_hbm, down)))
    ]

    def sum_cores(own, core_in, half, start_x):
        own[0:2 * half] += core_in[0:2 * half]
        start_x(0)
        start_x(1)
        own[2 * half:6 * half] += core_in[2 * half:6 * half]
        start_x(2)
        start_x(3)
        own[6 * half:8 * half] += core_in[6 * half:8 * half]

    def pass_on(own, far, far_recv, half, x_of):
        wait_bytes(far, far_recv)
        own[2 * half:3 * half] += far[0]
        x_of(4).start()
        own[5 * half:6 * half] += far[1]
        x_of(5).start()

    def total_of(own, near, half, rows, columns):
        return (
            own[6 * half + rows.start:6 * half + rows.stop, columns].astype(F32)
            + near[0, rows, columns].astype(F32)
            + near[1, rows, columns].astype(F32)
        ).astype(BF)

    def a_multiply(c):
        rot_copy(c).wait()
        if c + 1 < A_CHUNKS:
            rot_copy(c + 1).start()

        @pl.loop(0, A_WIDTHS[c] // TILE)
        def _(t):
            here = pl.ds(pl.multiple_of(t * TILE, TILE), TILE)
            there = pl.ds(pl.multiple_of(A_STARTS[c] + t * TILE, TILE), TILE)
            total = dot(lhs_a[...], rot[:, there])
            a_core_out[c][:, here] = total[:128].astype(BF)
            a_own[c][:, here] = total[128:].astype(BF)

    def a_sum_cores(c):
        a_core(c).wait_recv()
        sum_cores(a_own[c], a_core_in[c], 16, lambda i: a_x(c, i).start())

    def a_pass_on(c):
        pass_on(a_own[c], a_far[c], a_far_recv.at[c], 16, lambda i: a_x(c, i))

    def a_to_peers(c):
        wait_bytes(a_near[c], a_near_recv.at[c])
        eighth = A_WIDTHS[c] // 8
        for m in range(2):
            for q in range(8):
                a_sum[c][m * 8 + q] = total_of(
                    a_own[c], a_near[c], 16,
                    slice(m * 16, m * 16 + 16), slice(q * eighth, (q + 1) * eighth),
                )
        for i in range(OTHERS):
            a_spread(c, i).start()
        a_in[c][ep] = a_sum[c][ep]

    def a_to_owners(c):
        wait_bytes(a_in[c].at[pl.ds(0, OTHERS)], a_in_recv.at[c])
        eighth = A_WIDTHS[c] // 8
        rows = dot(sel_a[...], a_in[c][...].reshape(256, eighth))
        a_pick[c][...] = rows.astype(BF).reshape(16, 32, eighth)
        for i in range(OTHERS):
            a_owner(c, i).start()
        a_got[c][ep] = a_pick[c][ep]

    def a_place(c):
        wait_bytes(a_got[c].at[pl.ds(0, OTHERS)], a_own_recv.at[c])
        both = jnp.concatenate([
            jnp.concatenate([a_got[c][m * 8 + q] for q in range(8)], axis=1) for m in range(2)
        ], axis=0)
        a_out[:, pl.ds(A_STARTS[c], A_WIDTHS[c])] = dot(put_a[...], both).astype(BF)
        a_store(c).start()

    def multiply(width, start, core_out, own):
        total = dot(lhs_b[...], rot[:, pl.ds(start, width)])
        core_out[...] = total[:256].astype(BF)
        own[...] = total[256:].astype(BF)

    def pick_rows(width, own, near, pick):
        quarter = width // 4
        quarters = []
        for g in range(4):
            columns = slice(g * quarter, (g + 1) * quarter)
            quarters.append(jnp.concatenate([
                total_of(own, near, 32, slice(k * 32, k * 32 + 32), columns) for k in range(2)
            ], axis=1))
        rows = dot(sel_b[...], jnp.concatenate(quarters, axis=0))
        pick[...] = rows.astype(BF).reshape(16, 16, 2 * quarter)

    def b_multiply(n):
        start = pl.multiple_of(n * B_WIDTH, B_WIDTH)
        multiply(B_WIDTH, start, b_core_out.at[n], b_own.at[n])
        b_core(n).start()

    def b_sum_cores(n):
        b_core(n).wait_recv()
        sum_cores(b_own.at[n], b_core_in.at[n], 32, lambda i: b_x(n, i).start())

    def b_pass_on(n):
        pass_on(b_own.at[n], b_far.at[n], b_far_recv.at[n], 32, lambda i: b_x(n, i))

    def b_to_owners(n):
        wait_bytes(b_near.at[n], b_near_recv.at[n])
        pick_rows(B_WIDTH, b_own.at[n], b_near.at[n], b_pick.at[n])
        for i in range(OTHERS):
            b_owner(n, i).start()
        b_got[n, ep] = b_pick[n, ep]

    def b_place(n):
        wait_bytes(b_got.at[n, pl.ds(0, OTHERS)], b_own_recv.at[n])
        place_rows(put_b[...], b_got.at[n], b_out.at[n])
        b_store(n).start()

    def c_multiply(n):
        multiply(C_WIDTH, C_START + n * C_WIDTH, c_core_out[n], c_own[n])
        c_core(n).start()

    def c_sum_cores(n):
        c_core(n).wait_recv()
        sum_cores(c_own[n], c_core_in[n], 32, lambda i: c_x(n, i).start())

    def c_pass_on(n):
        pass_on(c_own[n], c_far[n], c_far_recv.at[n], 32, lambda i: c_x(n, i))

    def c_to_owners(n):
        wait_bytes(c_near[n], c_near_recv.at[n])
        pick_rows(C_WIDTH, c_own[n], c_near[n], c_pick[n])
        for i in reversed(range(OTHERS)):
            c_owner(n, i).start()
        if n < C_CHUNKS - 1:
            c_got[n][ep] = c_pick[n][ep]
        else:
            last_keep().start()

    def c_place(n):
        wait_bytes(c_got[n].at[pl.ds(0, OTHERS)], c_own_recv.at[n])
        place_rows(put_b[...], c_got[n], c_out.at[n])
        c_store(n).start()

    in_copies[0].start()
    rot_copy(0).start()
    in_copies[1].start()
    in_copies[2].start()

    r, s = iotas(256, 128)
    block = ((x + ring_offset((r // 32) % 4)) % 4) * 2 + jnp.where(r < 128, 1 - core, core)
    column = block * 16 + r % 16
    expert = (r // 16) % 2
    in_copies[0].wait()
    rows = sum(dot_t(onehot((expert == m) & (s == column)), gate[m]) for m in range(2))
    lhs_a[...] = rows.astype(BF)

    a_multiply(0)

    pl.semaphore_wait(barrier, 3 + OTHERS)

    a_core(0).start()
    column = (r % 8) * 16 + r // 16
    expert = (r // 8) % 2
    spread = [onehot((expert == m) & (s == column)) for m in range(2)]
    in_copies[1].wait()
    rows = sum(dot_t(spread[m], up[m]) for m in range(2))
    src[:, 0] = rows.astype(BF).reshape(16, 16, PIECE)
    in_copies[2].wait()
    rows = sum(dot(spread[m], down[m]) for m in range(2))
    src[:, 1] = rows.astype(BF).reshape(16, 16, PIECE)
    for i in range(OTHERS):
        src_copy(i).start()
    a_sum_cores(0)
    a_multiply(1)
    a_core(1).start()
    a_multiply(2)
    a_core(2).start()
    a_sum_cores(1)
    a_pass_on(0)
    a_multiply(3)
    a_core(3).start()
    a_sum_cores(2)
    a_pass_on(1)
    rcv[ep] = src[ep]
    low, high, mine = ranges(hid, ep, placement_ref, count_ref)
    sel_a[...] = select_a(ep, low, high)
    a_to_peers(0)
    a_sum_cores(3)
    a_pass_on(2)
    r, s = iotas(512, 512)
    block = ((x + ring_offset((r // 64) % 4)) % 4) * 2 + jnp.where(r < 256, 1 - core, core)
    arrange[...] = onehot(
        s == (r % 16) * 32 + ((r // 32) % 2) * 16 + ((r // 16) % 2) * 8 + block
    )
    put_a[...] = place_a(mine)
    put_b[...] = order_owner_rows()
    sel_b[...] = select_b(low, high)
    a_to_peers(1)
    a_pass_on(3)

    wait_bytes(rcv.at[pl.ds(0, OTHERS)], src_recv)
    lhs_b[...] = dot(arrange[...], rcv[...].reshape(512, PIECE)).astype(BF)
    b_multiply(0)
    a_to_owners(0)
    a_to_peers(2)

    stages = (
        (b_sum_cores, 0), (b_multiply, -1), (b_pass_on, 1), (b_to_owners, 2),
    )
    extras = {
        0: (lambda: a_to_owners(1), lambda: a_to_peers(3)),
        1: (lambda: a_to_owners(2),),
        2: (lambda: a_to_owners(3),),
        B_CHUNKS - 1: (lambda: c_multiply(0), lambda: c_multiply(1)),
    }

    @pl.loop(0, B_CHUNKS)
    def _(t):
        for stage, lag in stages:
            @pl.when((t >= lag) & (t < B_CHUNKS + lag))
            def _():
                stage(t - lag)
        for at, work in extras.items():
            @pl.when(t == at)
            def _():
                for one in work:
                    one()

    c_sum_cores(0)
    b_pass_on(B_CHUNKS - 1)
    c_sum_cores(1)
    a_place(0)
    a_place(1)
    b_to_owners(B_CHUNKS - 2)
    c_pass_on(0)
    a_place(2)
    a_place(3)
    b_to_owners(B_CHUNKS - 1)
    c_pass_on(1)
    b_place(0)
    b_place(1)
    c_to_owners(0)
    b_place(2)
    c_to_owners(1)
    for n in range(3, B_CHUNKS):
        b_place(n)
    c_place(0)

    rest = pl.ds(0, OTHERS)
    wait_bytes(src.at[rest], src_send)
    for c in range(A_CHUNKS):
        a_core(c).wait_send()
        wait_bytes(a_own[c].at[pl.ds(0, 96)], a_x_send.at[c])
        wait_bytes(a_sum[c].at[rest], a_in_send.at[c])
        wait_bytes(a_pick[c].at[rest], a_own_send.at[c])
        a_store(c).wait()
    wait_bytes(b_core_out, b_core_send)
    wait_bytes(b_own.at[:, pl.ds(0, 192)], b_x_send)
    wait_bytes(b_pick.at[:, rest], b_own_send)
    for n in range(C_CHUNKS):
        c_core(n).wait_send()
        wait_bytes(c_own[n].at[pl.ds(0, 192)], c_x_send.at[n])
        wait_bytes(c_pick[n].at[rest], c_own_send.at[n])
    last_keep().wait()
    wait_bytes(b_out, b_store_sem)
    c_store(0).wait()
    wait_bytes(last_got.at[rest], c_own_recv.at[C_CHUNKS - 1])


def place_kernel(part_hbm, last_got, out_hbm, got, held, load, got_load, store):
    last = HIDDEN - C_WIDTH
    pieces = [(pl.ds(0, 3), n * 1024, 1024) for n in range(last // 1024)]
    pieces.append((pl.ds(0, 3), last - last % 1024, last % 1024))
    pieces.append((pl.ds(0, 1), last, C_WIDTH))
    pieces = [(kinds, slice(None), pl.ds(start, width)) for kinds, start, width in pieces]
    loads = [
        pltpu.make_async_copy(part_hbm.at[at], held.at[at], load.at[i])
        for i, at in enumerate(pieces)
    ]
    pieces.append((pl.ds(1, 2), slice(None), pl.ds(last, C_WIDTH)))
    stores = [
        pltpu.make_async_copy(held.at[at], out_hbm.at[at], store.at[i])
        for i, at in enumerate(pieces)
    ]
    got_copy = pltpu.make_async_copy(last_got, got, got_load)
    got_copy.start()
    for copy in loads:
        copy.start()
    put_b = order_owner_rows()
    for load, store in zip(loads[:4], stores[:4]):
        load.wait()
        store.start()
    got_copy.wait()
    place_rows(put_b, got, held.at[pl.ds(1, 2), :, pl.ds(last, C_WIDTH)])
    stores[-1].start()
    for load, store in zip(loads[4:], stores[4:]):
        load.wait()
        store.start()
    for copy in stores:
        copy.wait()


def on_device(gate_proj, up_proj, down_proj, rotation, placement, row_count):
    dma = pltpu.SemaphoreType.DMA
    smem = pl.BlockSpec(memory_space=pltpu.SMEM)
    hbm = pl.BlockSpec(memory_space=pl.ANY)

    def held(*shape):
        return pltpu.VMEM(shape, BF)

    def per_a(shape_of):
        return [held(*shape_of(w)) for w in A_WIDTHS]

    b = B_CHUNKS
    c = C_CHUNKS
    one = dma
    each_a, each_b, each_c = dma((A_CHUNKS,)), dma((b,)), dma((c,))
    scratch = [
        held(*gate_proj.shape), held(*up_proj.shape), held(*down_proj.shape),
        held(PIECE, HIDDEN), held(256, PIECE), held(512, PIECE),
        held(16, 2, 16, PIECE), held(16, 2, 16, PIECE),
        held(512, 256), held(64, 64), held(256, 128), held(256, 256), held(512, 512),
        *per_a(lambda w: (128, w)),
        *per_a(lambda w: (128, w)),
        *per_a(lambda w: (128, w)),
        *per_a(lambda w: (2, 16, w)),
        *per_a(lambda w: (2, 32, w)),
        *per_a(lambda w: (16, 16, w // 8)),
        *per_a(lambda w: (16, 16, w // 8)),
        *per_a(lambda w: (16, 32, w // 8)),
        *per_a(lambda w: (16, 32, w // 8)),
        held(b, 256, B_WIDTH), held(b, 256, B_WIDTH), held(b, 256, B_WIDTH),
        held(b, 2, 32, B_WIDTH), held(b, 2, 64, B_WIDTH),
        held(b, 16, 16, B_WIDTH // 2), held(b, 16, 16, B_WIDTH // 2),
        *[held(256, C_WIDTH)] * (3 * c),
        *[held(2, 32, C_WIDTH)] * c, *[held(2, 64, C_WIDTH)] * c, *[held(16, 16, C_WIDTH // 2)] * c,
        *[held(16, 16, C_WIDTH // 2)] * (c - 1),
        held(64, HIDDEN), held(b, 2, 64, B_WIDTH), held(c, 2, 64, C_WIDTH),
        dma((3,)), each_a, one, one,
        each_a, one, each_c,
        *[each_a] * 9,
        one, each_b, one, each_b, each_b,
        one, each_b,
        *[each_c] * 7, one,
    ]
    arrived = [
        jax.ShapeDtypeStruct((3, 64, HIDDEN), BF),
        jax.ShapeDtypeStruct((16, 16, C_WIDTH // 2), BF),
    ]
    part, last_got = pl.pallas_call(
        kernel,
        out_shape=arrived,
        in_specs=[smem, smem, hbm, hbm, hbm, hbm],
        out_specs=[hbm] * len(arrived),
        scratch_shapes=scratch,
        compiler_params=pltpu.CompilerParams(
            collective_id=0, has_side_effects=True, vmem_limit_bytes=56 * 1024 * 1024
        ),
        name="rotate_and_send",
    )(placement, row_count, gate_proj, up_proj, down_proj, rotation)
    out = pl.pallas_call(
        place_kernel,
        out_shape=jax.ShapeDtypeStruct((3, 64, HIDDEN), BF),
        in_specs=[hbm] * 2,
        out_specs=hbm,
        scratch_shapes=[
            held(16, 16, C_WIDTH // 2), held(3, 64, HIDDEN), dma((9,)), one, dma((10,)),
        ],
        compiler_params=pltpu.CompilerParams(vmem_limit_bytes=60 * 1024 * 1024),
        name="place",
    )(part, last_got)
    return jnp.transpose(out, (1, 0, 2))[None]


def solution(mesh):
    in_specs = (
        P(None, "hid", "ep"),
        P(None, "hid", "ep"),
        P(None, "ep", "hid"),
        P("hid", None),
        P(),
        P(),
    )
    out_specs = P("ep", "hid", None, None)
    return jax.shard_map(
        on_device, mesh=mesh, in_specs=in_specs, out_specs=out_specs, check_vma=False
    )
```

```python
import jax
import jax.numpy as jnp
from jax import lax
from jax.experimental import pallas as pl
from jax.experimental.pallas import tpu as pltpu
from jax.sharding import PartitionSpec as P

MESH = pl.DeviceIdType.MESH
BF = jnp.bfloat16
F32 = jnp.float32
PEERS = (
    (0, 1), (0, 3), (1, 0), (3, 0), (1, 1), (3, 3), (1, 3), (3, 1),
    (0, 2), (2, 0), (1, 2), (2, 1), (3, 2), (2, 3), (2, 2),
)
OTHERS = len(PEERS)
HIDDEN = 7168
PIECE = 896
A_WIDTHS = (1024, 2048, 2048, 2048)
A_STARTS = (0, 1024, 3072, 5120)
A_CHUNKS = len(A_WIDTHS)
B_WIDTH = 1024
B_CHUNKS = 6
C_WIDTH = 512
C_START = B_CHUNKS * B_WIDTH
C_CHUNKS = (HIDDEN - C_START) // C_WIDTH
TILE = 1024


def iotas(rows, cols):
    return (
        lax.broadcasted_iota(jnp.int32, (rows, cols), 0),
        lax.broadcasted_iota(jnp.int32, (rows, cols), 1),
    )


def onehot(condition):
    return jnp.where(condition, 1.0, 0.0).astype(BF)


def dot(a, b):
    return jnp.dot(a, b, preferred_element_type=F32)


def dot_t(a, b):
    return lax.dot_general(a, b, (((1,), (1,)), ((), ())), preferred_element_type=F32)


def ring_offset(index):
    return jnp.where(index == 0, 2, jnp.where(index == 1, 1, jnp.where(index == 2, 3, 0)))


def ranges(h, ep, placement_ref, count_ref):
    owners, _ = iotas(16, 256)
    low, high, mine = [], [], []
    for m in range(2):
        start = jnp.int32(0)
        count = jnp.int32(0)
        lo = jnp.zeros((16, 256), jnp.int32)
        hi = jnp.zeros((16, 256), jnp.int32)
        for t in range(16):
            o = placement_ref[m, t]
            end = start + lax.shift_right_logical(count_ref[m, o], 4)
            first = lax.shift_right_logical(start + 7 - h, 3)
            last = lax.shift_right_logical(end + 7 - h, 3)
            lo = jnp.where(owners == o, first, lo)
            hi = jnp.where(owners == o, last, hi)
            count = jnp.where(o == ep, last - first, count)
            start = end
        low.append(lo)
        high.append(hi)
        mine.append(count)
    return low, high, mine


def select_a(ep, low, high):
    first = ep < 8
    lo = jnp.where(first, low[0], low[1])
    hi = jnp.where(first, high[0], high[1])
    _, col = iotas(16, 256)
    e = col // 16
    place = jnp.where((lo <= e) & (e < hi), e - lo, -1)
    place = jnp.broadcast_to(place[:, None, :], (16, 32, 256)).reshape(512, 256)
    r, s = iotas(512, 256)
    return onehot((place == (r // 16) % 2) & (r % 16 == s % 16))


def place_a(mine):
    r, s = iotas(64, 64)
    slot = (s // 16) % 2 + jnp.where(s < 32, 0, mine[0])
    return onehot((slot == r // 16) & (r % 16 == s % 16))


def select_b(low, high):
    _, col = iotas(16, 128)
    m = (col // 16) % 2
    e = col % 16
    low = [v[:, :128] for v in low]
    high = [v[:, :128] for v in high]
    lo = jnp.where(m == 0, low[0], low[1])
    hi = jnp.where(m == 0, high[0], high[1])
    slot = e - lo + jnp.where(m == 0, 0, high[0] - low[0])
    slot = jnp.where((lo <= e) & (e < hi), slot, -1)
    slot = jnp.broadcast_to(slot[:, None, :], (16, 16, 128)).reshape(256, 128)
    r, s = iotas(256, 128)
    return onehot((slot == (r // 4) % 4) & (r % 4 == s // 32))


def order_owner_rows():
    r, s = iotas(256, 256)
    return onehot(s == (r % 16) * 16 + ((r // 16) % 4) * 4 + r // 64)


def place_rows(put_b, got, out):
    width = got.shape[-1] // 2
    rows = dot(put_b, got[...].reshape(256, 2 * width)).astype(BF)
    for k in range(2):
        for g in range(4):
            out[k, :, g * width:(g + 1) * width] = rows[
                g * 64:(g + 1) * 64, k * width:(k + 1) * width
            ]


def kernel(
    placement_ref, count_ref, gate_hbm, up_hbm, down_hbm, rot_hbm, *scratch
):
    scratch = list(scratch)

    def take(count):
        taken = scratch[:count]
        del scratch[:count]
        return taken

    part_hbm, last_got = take(2)
    gate, up, down = take(3)
    rot, lhs_a, lhs_b, src, rcv, sel_a, put_a, sel_b, put_b, arrange = take(10)
    a_core_out, a_core_in, a_own, a_far, a_near, a_sum, a_in, a_pick, a_got = (
        take(A_CHUNKS) for _ in range(9)
    )
    b_core_out, b_core_in, b_own, b_far, b_near, b_pick, b_got = take(7)
    c_core_out, c_core_in, c_own, c_far, c_near, c_pick = (take(C_CHUNKS) for _ in range(6))
    c_got = take(C_CHUNKS - 1) + [last_got]
    a_out, b_out, c_out = take(3)
    in_sem, rot_sem, src_send, src_recv = take(4)
    a_store_sem, b_store_sem, c_store_sem = take(3)
    a_core_send, a_core_recv, a_x_send, a_far_recv, a_near_recv = take(5)
    a_in_send, a_in_recv, a_own_send, a_own_recv = take(4)
    b_core_send, b_core_recv, b_x_send, b_far_recv, b_near_recv = take(5)
    b_own_send, b_own_recv = take(2)
    c_core_send, c_core_recv, c_x_send, c_far_recv, c_near_recv = take(5)
    c_own_send, c_own_recv, c_self = take(3)

    hid = lax.axis_index("hid")
    ep = lax.axis_index("ep")
    x, core = hid // 2, hid % 2
    z, y = ep // 4, ep % 4
    right = lax.rem(x + 1, 4) * 2 + core
    left = lax.rem(x + 3, 4) * 2 + core
    other = x * 2 + 1 - core
    peers = [lax.rem(z + dz, 4) * 4 + lax.rem(y + dy, 4) for dz, dy in PEERS]

    def remote(source, target, send, recv, h, e):
        return pltpu.make_async_remote_copy(
            source, target, send, recv, device_id=(h, e), device_id_type=MESH
        )

    def wait_bytes(ref, sem):
        pltpu.make_async_copy(ref, ref, sem).wait()

    barrier = pltpu.get_barrier_semaphore()
    for h in (right, left, other):
        pl.semaphore_signal(barrier, 1, device_id=(h, ep), device_id_type=MESH)
    for p in peers:
        pl.semaphore_signal(barrier, 1, device_id=(hid, p), device_id_type=MESH)

    def rot_copy(c):
        columns = pl.ds(A_STARTS[c], A_WIDTHS[c])
        return pltpu.make_async_copy(rot_hbm.at[:, columns], rot.at[:, columns], rot_sem.at[c])

    def src_copy(i):
        return remote(
            src.at[peers[i]], rcv.at[ep], src_send, src_recv, hid, peers[i]
        )

    def x_copy(own, far, near, send, far_recv, near_recv, half, i):
        first, to, target, recv = (
            (0, right, far.at[0], far_recv),
            (1, left, far.at[1], far_recv),
            (3, right, near.at[0, pl.ds(half, half)], near_recv),
            (4, left, near.at[1, pl.ds(0, half)], near_recv),
            (2, right, near.at[0, pl.ds(0, half)], near_recv),
            (5, left, near.at[1, pl.ds(half, half)], near_recv),
        )[i]
        return remote(own.at[pl.ds(first * half, half)], target, send, recv, to, ep)

    def a_x(c, i):
        return x_copy(
            a_own[c], a_far[c], a_near[c],
            a_x_send.at[c], a_far_recv.at[c], a_near_recv.at[c], 16, i,
        )

    def b_x(n, i):
        return x_copy(
            b_own.at[n], b_far.at[n], b_near.at[n],
            b_x_send, b_far_recv.at[n], b_near_recv.at[n], 32, i,
        )

    def c_x(n, i):
        return x_copy(
            c_own[n], c_far[n], c_near[n],
            c_x_send.at[n], c_far_recv.at[n], c_near_recv.at[n], 32, i,
        )

    def c_core(n):
        return remote(c_core_out[n], c_core_in[n], c_core_send.at[n], c_core_recv.at[n], other, ep)

    def c_owner(n, i):
        return remote(
            c_pick[n].at[peers[i]], c_got[n].at[ep], c_own_send.at[n], c_own_recv.at[n],
            hid, peers[i],
        )

    def last_keep():
        return pltpu.make_async_copy(c_pick[-1].at[ep], last_got.at[ep], c_self)

    def a_core(c):
        return remote(a_core_out[c], a_core_in[c], a_core_send.at[c], a_core_recv.at[c], other, ep)

    def b_core(n):
        return remote(
            b_core_out.at[n], b_core_in.at[n], b_core_send, b_core_recv.at[n], other, ep
        )

    def a_spread(c, i):
        return remote(
            a_sum[c].at[peers[i]], a_in[c].at[ep], a_in_send.at[c], a_in_recv.at[c], hid, peers[i]
        )

    def a_owner(c, i):
        return remote(
            a_pick[c].at[peers[i]], a_got[c].at[ep], a_own_send.at[c], a_own_recv.at[c],
            hid, peers[i],
        )

    def b_owner(n, i):
        return remote(
            b_pick.at[n, peers[i]], b_got.at[n, ep], b_own_send, b_own_recv.at[n], hid, peers[i]
        )

    def a_store(c):
        columns = pl.ds(A_STARTS[c], A_WIDTHS[c])
        return pltpu.make_async_copy(
            a_out.at[:, columns], part_hbm.at[0, :, columns], a_store_sem.at[c]
        )

    def b_store(n):
        columns = pl.ds(pl.multiple_of(n * B_WIDTH, B_WIDTH), B_WIDTH)
        return pltpu.make_async_copy(
            b_out.at[n], part_hbm.at[pl.ds(1, 2), :, columns], b_store_sem
        )

    def c_store(n):
        columns = pl.ds(C_START + n * C_WIDTH, C_WIDTH)
        return pltpu.make_async_copy(
            c_out.at[n], part_hbm.at[pl.ds(1, 2), :, columns], c_store_sem.at[n]
        )

    in_copies = [
        pltpu.make_async_copy(source, target, in_sem.at[i])
        for i, (source, target) in enumerate(((gate_hbm, gate), (up_hbm, up), (down_hbm, down)))
    ]

    def sum_cores(own, core_in, half, start_x):
        own[0:2 * half] += core_in[0:2 * half]
        start_x(0)
        start_x(1)
        own[2 * half:6 * half] += core_in[2 * half:6 * half]
        start_x(2)
        start_x(3)
        own[6 * half:8 * half] += core_in[6 * half:8 * half]

    def pass_on(own, far, far_recv, half, x_of):
        wait_bytes(far, far_recv)
        own[2 * half:3 * half] += far[0]
        x_of(4).start()
        own[5 * half:6 * half] += far[1]
        x_of(5).start()

    def total_of(own, near, half, rows, columns):
        return (
            own[6 * half + rows.start:6 * half + rows.stop, columns].astype(F32)
            + near[0, rows, columns].astype(F32)
            + near[1, rows, columns].astype(F32)
        ).astype(BF)

    def a_multiply(c):
        rot_copy(c).wait()
        if c + 1 < A_CHUNKS:
            rot_copy(c + 1).start()

        @pl.loop(0, A_WIDTHS[c] // TILE)
        def _(t):
            here = pl.ds(pl.multiple_of(t * TILE, TILE), TILE)
            there = pl.ds(pl.multiple_of(A_STARTS[c] + t * TILE, TILE), TILE)
            total = dot(lhs_a[...], rot[:, there])
            a_core_out[c][:, here] = total[:128].astype(BF)
            a_own[c][:, here] = total[128:].astype(BF)

    def a_sum_cores(c):
        a_core(c).wait_recv()
        sum_cores(a_own[c], a_core_in[c], 16, lambda i: a_x(c, i).start())

    def a_pass_on(c):
        pass_on(a_own[c], a_far[c], a_far_recv.at[c], 16, lambda i: a_x(c, i))

    def a_to_peers(c):
        wait_bytes(a_near[c], a_near_recv.at[c])
        eighth = A_WIDTHS[c] // 8
        for m in range(2):
            for q in range(8):
                a_sum[c][m * 8 + q] = total_of(
                    a_own[c], a_near[c], 16,
                    slice(m * 16, m * 16 + 16), slice(q * eighth, (q + 1) * eighth),
                )
        for i in range(OTHERS):
            a_spread(c, i).start()
        a_in[c][ep] = a_sum[c][ep]

    def a_to_owners(c):
        wait_bytes(a_in[c].at[pl.ds(0, OTHERS)], a_in_recv.at[c])
        eighth = A_WIDTHS[c] // 8
        rows = dot(sel_a[...], a_in[c][...].reshape(256, eighth))
        a_pick[c][...] = rows.astype(BF).reshape(16, 32, eighth)
        for i in range(OTHERS):
            a_owner(c, i).start()
        a_got[c][ep] = a_pick[c][ep]

    def a_place(c):
        wait_bytes(a_got[c].at[pl.ds(0, OTHERS)], a_own_recv.at[c])
        both = jnp.concatenate([
            jnp.concatenate([a_got[c][m * 8 + q] for q in range(8)], axis=1) for m in range(2)
        ], axis=0)
        a_out[:, pl.ds(A_STARTS[c], A_WIDTHS[c])] = dot(put_a[...], both).astype(BF)
        a_store(c).start()

    def multiply(width, start, core_out, own):
        total = dot(lhs_b[...], rot[:, pl.ds(start, width)])
        core_out[...] = total[:256].astype(BF)
        own[...] = total[256:].astype(BF)

    def pick_rows(width, own, near, pick):
        quarter = width // 4
        quarters = []
        for g in range(4):
            columns = slice(g * quarter, (g + 1) * quarter)
            quarters.append(jnp.concatenate([
                total_of(own, near, 32, slice(k * 32, k * 32 + 32), columns) for k in range(2)
            ], axis=1))
        rows = dot(sel_b[...], jnp.concatenate(quarters, axis=0))
        pick[...] = rows.astype(BF).reshape(16, 16, 2 * quarter)

    def b_multiply(n):
        start = pl.multiple_of(n * B_WIDTH, B_WIDTH)
        multiply(B_WIDTH, start, b_core_out.at[n], b_own.at[n])
        b_core(n).start()

    def b_sum_cores(n):
        b_core(n).wait_recv()
        sum_cores(b_own.at[n], b_core_in.at[n], 32, lambda i: b_x(n, i).start())

    def b_pass_on(n):
        pass_on(b_own.at[n], b_far.at[n], b_far_recv.at[n], 32, lambda i: b_x(n, i))

    def b_to_owners(n):
        wait_bytes(b_near.at[n], b_near_recv.at[n])
        pick_rows(B_WIDTH, b_own.at[n], b_near.at[n], b_pick.at[n])
        for i in range(OTHERS):
            b_owner(n, i).start()
        b_got[n, ep] = b_pick[n, ep]

    def b_place(n):
        wait_bytes(b_got.at[n, pl.ds(0, OTHERS)], b_own_recv.at[n])
        place_rows(put_b[...], b_got.at[n], b_out.at[n])
        b_store(n).start()

    def c_multiply(n):
        multiply(C_WIDTH, C_START + n * C_WIDTH, c_core_out[n], c_own[n])
        c_core(n).start()

    def c_sum_cores(n):
        c_core(n).wait_recv()
        sum_cores(c_own[n], c_core_in[n], 32, lambda i: c_x(n, i).start())

    def c_pass_on(n):
        pass_on(c_own[n], c_far[n], c_far_recv.at[n], 32, lambda i: c_x(n, i))

    def c_to_owners(n):
        wait_bytes(c_near[n], c_near_recv.at[n])
        pick_rows(C_WIDTH, c_own[n], c_near[n], c_pick[n])
        for i in reversed(range(OTHERS)):
            c_owner(n, i).start()
        if n < C_CHUNKS - 1:
            c_got[n][ep] = c_pick[n][ep]
        else:
            last_keep().start()

    def c_place(n):
        wait_bytes(c_got[n].at[pl.ds(0, OTHERS)], c_own_recv.at[n])
        place_rows(put_b[...], c_got[n], c_out.at[n])
        c_store(n).start()

    in_copies[0].start()
    rot_copy(0).start()
    in_copies[1].start()
    in_copies[2].start()

    r, s = iotas(256, 128)
    block = ((x + ring_offset((r // 32) % 4)) % 4) * 2 + jnp.where(r < 128, 1 - core, core)
    column = block * 16 + r % 16
    expert = (r // 16) % 2
    in_copies[0].wait()
    rows = sum(dot_t(onehot((expert == m) & (s == column)), gate[m]) for m in range(2))
    lhs_a[...] = rows.astype(BF)

    a_multiply(0)

    pl.semaphore_wait(barrier, 3 + OTHERS)

    a_core(0).start()
    column = (r % 8) * 16 + r // 16
    expert = (r // 8) % 2
    spread = [onehot((expert == m) & (s == column)) for m in range(2)]
    in_copies[1].wait()
    rows = sum(dot_t(spread[m], up[m]) for m in range(2))
    src[:, 0] = rows.astype(BF).reshape(16, 16, PIECE)
    in_copies[2].wait()
    rows = sum(dot(spread[m], down[m]) for m in range(2))
    src[:, 1] = rows.astype(BF).reshape(16, 16, PIECE)
    for i in range(OTHERS):
        src_copy(i).start()
    a_sum_cores(0)
    a_multiply(1)
    a_core(1).start()
    a_multiply(2)
    a_core(2).start()
    a_sum_cores(1)
    a_pass_on(0)
    a_multiply(3)
    a_core(3).start()
    a_sum_cores(2)
    a_pass_on(1)
    rcv[ep] = src[ep]
    low, high, mine = ranges(hid, ep, placement_ref, count_ref)
    sel_a[...] = select_a(ep, low, high)
    a_to_peers(0)
    a_sum_cores(3)
    a_pass_on(2)
    r, s = iotas(512, 512)
    block = ((x + ring_offset((r // 64) % 4)) % 4) * 2 + jnp.where(r < 256, 1 - core, core)
    arrange[...] = onehot(
        s == (r % 16) * 32 + ((r // 32) % 2) * 16 + ((r // 16) % 2) * 8 + block
    )
    put_a[...] = place_a(mine)
    put_b[...] = order_owner_rows()
    sel_b[...] = select_b(low, high)
    a_to_peers(1)
    a_pass_on(3)

    wait_bytes(rcv.at[pl.ds(0, OTHERS)], src_recv)
    lhs_b[...] = dot(arrange[...], rcv[...].reshape(512, PIECE)).astype(BF)
    b_multiply(0)
    a_to_owners(0)
    a_to_peers(2)

    stages = (
        (b_sum_cores, 0), (b_pass_on, 1), (b_multiply, -1), (b_to_owners, 2),
    )
    extras = {
        0: (lambda: a_to_owners(1), lambda: a_to_peers(3)),
        1: (lambda: a_to_owners(2),),
        2: (lambda: a_to_owners(3),),
        B_CHUNKS - 1: (lambda: c_multiply(0), lambda: c_multiply(1)),
    }

    @pl.loop(0, B_CHUNKS)
    def _(t):
        for stage, lag in stages:
            @pl.when((t >= lag) & (t < B_CHUNKS + lag))
            def _():
                stage(t - lag)
        for at, work in extras.items():
            @pl.when(t == at)
            def _():
                for one in work:
                    one()

    c_sum_cores(0)
    b_pass_on(B_CHUNKS - 1)
    c_sum_cores(1)
    a_place(0)
    a_place(1)
    b_to_owners(B_CHUNKS - 2)
    c_pass_on(0)
    a_place(2)
    a_place(3)
    b_to_owners(B_CHUNKS - 1)
    c_pass_on(1)
    b_place(0)
    b_place(1)
    c_to_owners(0)
    b_place(2)
    c_to_owners(1)
    for n in range(3, B_CHUNKS):
        b_place(n)
    c_place(0)

    rest = pl.ds(0, OTHERS)
    wait_bytes(src.at[rest], src_send)
    for c in range(A_CHUNKS):
        a_core(c).wait_send()
        wait_bytes(a_own[c].at[pl.ds(0, 96)], a_x_send.at[c])
        wait_bytes(a_sum[c].at[rest], a_in_send.at[c])
        wait_bytes(a_pick[c].at[rest], a_own_send.at[c])
        a_store(c).wait()
    wait_bytes(b_core_out, b_core_send)
    wait_bytes(b_own.at[:, pl.ds(0, 192)], b_x_send)
    wait_bytes(b_pick.at[:, rest], b_own_send)
    for n in range(C_CHUNKS):
        c_core(n).wait_send()
        wait_bytes(c_own[n].at[pl.ds(0, 192)], c_x_send.at[n])
        wait_bytes(c_pick[n].at[rest], c_own_send.at[n])
    last_keep().wait()
    wait_bytes(b_out, b_store_sem)
    c_store(0).wait()
    wait_bytes(last_got.at[rest], c_own_recv.at[C_CHUNKS - 1])


def place_kernel(part_hbm, last_got, out_hbm, got, held, load, got_load, store):
    last = HIDDEN - C_WIDTH
    pieces = [(pl.ds(0, 3), n * 1024, 1024) for n in range(last // 1024)]
    pieces.append((pl.ds(0, 3), last - last % 1024, last % 1024))
    pieces.append((pl.ds(0, 1), last, C_WIDTH))
    pieces = [(kinds, slice(None), pl.ds(start, width)) for kinds, start, width in pieces]
    loads = [
        pltpu.make_async_copy(part_hbm.at[at], held.at[at], load.at[i])
        for i, at in enumerate(pieces)
    ]
    pieces.append((pl.ds(1, 2), slice(None), pl.ds(last, C_WIDTH)))
    stores = [
        pltpu.make_async_copy(held.at[at], out_hbm.at[at], store.at[i])
        for i, at in enumerate(pieces)
    ]
    got_copy = pltpu.make_async_copy(last_got, got, got_load)
    got_copy.start()
    for copy in loads:
        copy.start()
    put_b = order_owner_rows()
    for load, store in zip(loads[:4], stores[:4]):
        load.wait()
        store.start()
    got_copy.wait()
    place_rows(put_b, got, held.at[pl.ds(1, 2), :, pl.ds(last, C_WIDTH)])
    stores[-1].start()
    for load, store in zip(loads[4:], stores[4:]):
        load.wait()
        store.start()
    for copy in stores:
        copy.wait()


def on_device(gate_proj, up_proj, down_proj, rotation, placement, row_count):
    dma = pltpu.SemaphoreType.DMA
    smem = pl.BlockSpec(memory_space=pltpu.SMEM)
    hbm = pl.BlockSpec(memory_space=pl.ANY)

    def held(*shape):
        return pltpu.VMEM(shape, BF)

    def per_a(shape_of):
        return [held(*shape_of(w)) for w in A_WIDTHS]

    b = B_CHUNKS
    c = C_CHUNKS
    one = dma
    each_a, each_b, each_c = dma((A_CHUNKS,)), dma((b,)), dma((c,))
    scratch = [
        held(*gate_proj.shape), held(*up_proj.shape), held(*down_proj.shape),
        held(PIECE, HIDDEN), held(256, PIECE), held(512, PIECE),
        held(16, 2, 16, PIECE), held(16, 2, 16, PIECE),
        held(512, 256), held(64, 64), held(256, 128), held(256, 256), held(512, 512),
        *per_a(lambda w: (128, w)),
        *per_a(lambda w: (128, w)),
        *per_a(lambda w: (128, w)),
        *per_a(lambda w: (2, 16, w)),
        *per_a(lambda w: (2, 32, w)),
        *per_a(lambda w: (16, 16, w // 8)),
        *per_a(lambda w: (16, 16, w // 8)),
        *per_a(lambda w: (16, 32, w // 8)),
        *per_a(lambda w: (16, 32, w // 8)),
        held(b, 256, B_WIDTH), held(b, 256, B_WIDTH), held(b, 256, B_WIDTH),
        held(b, 2, 32, B_WIDTH), held(b, 2, 64, B_WIDTH),
        held(b, 16, 16, B_WIDTH // 2), held(b, 16, 16, B_WIDTH // 2),
        *[held(256, C_WIDTH)] * (3 * c),
        *[held(2, 32, C_WIDTH)] * c, *[held(2, 64, C_WIDTH)] * c, *[held(16, 16, C_WIDTH // 2)] * c,
        *[held(16, 16, C_WIDTH // 2)] * (c - 1),
        held(64, HIDDEN), held(b, 2, 64, B_WIDTH), held(c, 2, 64, C_WIDTH),
        dma((3,)), each_a, one, one,
        each_a, one, each_c,
        *[each_a] * 9,
        one, each_b, one, each_b, each_b,
        one, each_b,
        *[each_c] * 7, one,
    ]
    arrived = [
        jax.ShapeDtypeStruct((3, 64, HIDDEN), BF),
        jax.ShapeDtypeStruct((16, 16, C_WIDTH // 2), BF),
    ]
    part, last_got = pl.pallas_call(
        kernel,
        out_shape=arrived,
        in_specs=[smem, smem, hbm, hbm, hbm, hbm],
        out_specs=[hbm] * len(arrived),
        scratch_shapes=scratch,
        compiler_params=pltpu.CompilerParams(
            collective_id=0, has_side_effects=True, vmem_limit_bytes=56 * 1024 * 1024
        ),
        name="rotate_and_send",
    )(placement, row_count, gate_proj, up_proj, down_proj, rotation)
    out = pl.pallas_call(
        place_kernel,
        out_shape=jax.ShapeDtypeStruct((3, 64, HIDDEN), BF),
        in_specs=[hbm] * 2,
        out_specs=hbm,
        scratch_shapes=[
            held(16, 16, C_WIDTH // 2), held(3, 64, HIDDEN), dma((9,)), one, dma((10,)),
        ],
        compiler_params=pltpu.CompilerParams(vmem_limit_bytes=60 * 1024 * 1024),
        name="place",
    )(part, last_got)
    return jnp.transpose(out, (1, 0, 2))[None]


def solution(mesh):
    in_specs = (
        P(None, "hid", "ep"),
        P(None, "hid", "ep"),
        P(None, "ep", "hid"),
        P("hid", None),
        P(),
        P(),
    )
    out_specs = P("ep", "hid", None, None)
    return jax.shard_map(
        on_device, mesh=mesh, in_specs=in_specs, out_specs=out_specs, check_vma=False
    )
```
